256 devices in a mesh: dp: 16 (over z, core), expert: 4 (over x), tensor: 4 (over y).
Axes of the slice: x: 4, y: 4, z: 8, core: 2. Of those that a mesh axis runs over, the one named last changes fastest.
Arguments:
- tokens: bfloat16 [8192, 2048], P(('dp', 'expert', 'tensor')), may hold values from -6 to 6
- out_grad: bfloat16 [8192, 2048], P(('dp', 'expert', 'tensor')), may hold values from -6 to 6
- routes: int32 [8192, 6], P(('dp', 'expert', 'tensor')), may hold values from 0 to 63, all different within a row; in each aligned block of 32 rows (0 to 31, 32 to 63, ...) at most 4 rows name the same one
- gates: bfloat16 [8192, 6], P(('dp', 'expert', 'tensor')), may hold values from 0.099609375 to 1
- w_gate: bfloat16 [64, 2048, 1408], P(('dp', 'expert'), None, 'tensor'), may hold values from -0.125 to 0.125
- w_up: bfloat16 [64, 2048, 1408], P(('dp', 'expert'), None, 'tensor'), may hold values from -0.125 to 0.125
- w_down: bfloat16 [64, 1408, 2048], P(('dp', 'expert'), 'tensor'), may hold values from -0.15625 to 0.15625
Outputs:
- grad_tokens: bfloat16 [8192, 2048], P(('dp', 'expert', 'tensor'))
- grad_gate: bfloat16 [8192, 6], P(('dp', 'expert', 'tensor'))
- grad_down: float32 [64, 1408, 2048], P(('dp', 'expert'), 'tensor')
The draws below stay inside these ranges and needn't reach their ends.
Inputs may be any that keep to these rules, and one draw needn't show every extreme that they name: `routes`: each row names 6 different experts. In each device's block of 32 rows no expert is named more than 4 times, and in some block an expert is named exactly 4 times.
All inputs are finite; a program needn't handle non-finite values.
Results may differ from the reference program's by a relative error of at most 0.0057.
Values may be sent and summed in bfloat16 or wider, within the bound.
A program may use at most 128 MiB of HBM per device.

```python
import math
import jax
import jax.numpy as jnp
import numpy as np
from jax import lax

D = 2048
FF = 1408
TOP = 6
TOK_DEV = 32
EXPERTS = 64
CAP = 4
TOKENS = 8192
N_DP = 16
N_EXPERT = 4
N_TENSOR = 4


def steps_of(rng, extent, shards, low, largest):
    loudness = 1.0
    for axis_at, shards_of in shards:
        heights = jax.random.uniform(jax.random.fold_in(jax.random.fold_in(rng, 6), axis_at), (shards_of,), jnp.float32, low / len(shards), largest / len(shards))
        loudness = loudness * jnp.repeat(jnp.exp(heights), extent[axis_at] // shards_of).reshape((-1,) + (1,) * (len(extent) - 1 - axis_at))
    return loudness


def shared_out(key, own, number, rows, number_of, top, reach, slope):
    order = jax.random.permutation(key, number_of)
    heavy_load, common = shares(number_of, rows * top, reach, slope, True), shares(number_of, rows * top, reach, slope, False)
    places = jnp.arange(number_of)

    def named(lengths, turn):
        used = int((lengths > 0).sum())
        fixed = max(1, used // 4)
        passed = fixed + (places - fixed + turn * (used - fixed)) % max(1, number_of - fixed)
        return jnp.zeros((number_of,), jnp.int32).at[order[jnp.where(places < fixed, places, passed)]].set(jnp.asarray(lengths, jnp.int32))

    lengths = jnp.where(number % 4 == 0, named(heavy_load, number // 4), named(common, number - number // 4 - 1))
    mixed = jax.random.permutation(jax.random.fold_in(own, 3), number_of)
    source_of, receiver = mixed[0:number_of // 2 * 2:2], mixed[1:number_of // 2 * 2:2]
    margin = jnp.minimum(lengths[source_of] - 1, reach - lengths[receiver]) // 2
    margin = jnp.where((source_of == order[0]) | (receiver == order[0]) | (lengths[receiver] == 0), 0, jnp.maximum(margin, 0))
    passed = jax.random.randint(jax.random.fold_in(own, 4), (number_of // 2,), 0, 1 << 20) % (margin + 1)
    lengths = lengths.at[source_of].add(-passed).at[receiver].add(passed)
    labels = jnp.searchsorted(jnp.cumsum(lengths), jnp.arange(rows * top), side="right").astype(jnp.int32)
    grid = labels.reshape(top, rows).T
    grid = grid[jax.random.permutation(jax.random.fold_in(own, 1), rows)]
    turn = jax.random.randint(jax.random.fold_in(own, 2), (rows, 1), 0, top)
    return jnp.take_along_axis(grid, (jnp.arange(top)[None, :] + turn) % top, axis=1)


def shares(number_of, total, limit, skew, full):
    portions = [(1 << 20) // math.isqrt(standing ** skew) + 1 for standing in range(1, number_of + 1)]
    largest = limit if full else min(limit, max(-(-total // number_of), total * portions[0] // sum(portions)))
    least = 1 if total - largest >= number_of - 1 else 0
    holding, surplus = [largest] + [least] * (number_of - 1), total - largest - least * (number_of - 1)
    while surplus > 0:
        movable = [i for i in range(1, number_of) if holding[i] < largest] or [i for i in range(1, number_of) if holding[i] < limit]
        pool, left = sum([portions[i] for i in movable]), surplus
        for i in movable:
            more = min(limit - holding[i], max(1, left * portions[i] // pool), surplus)
            holding[i] = holding[i] + more
            surplus = surplus - more
    return np.array(holding)


def noise(stream_key, extent, scale, bound, shards=(), kind=jnp.bfloat16):
    gain = steps_of(stream_key, extent, shards, -0.22, 0.18) if shards else 1.0
    entries = jax.random.normal(stream_key, extent, jnp.float32) * scale * gain
    return jnp.minimum(jnp.maximum(entries, -bound), bound).astype(kind)


def setup_inputs(seed: int = 0) -> dict:
    splits = jax.random.split(jax.random.key(seed), 8)
    tokens = noise(splits[0], (TOKENS, D), 1.0, 6.0, ((0, 256),))
    out_grad = noise(splits[1], (TOKENS, D), 1.0, 6.0, ((0, 256),))
    routes_keys = jax.random.split(jax.random.fold_in(splits[2], 1), TOKENS // TOK_DEV)
    routes_turns = jax.random.permutation(jax.random.fold_in(splits[2], 3), TOKENS // TOK_DEV)
    routes = jax.vmap(lambda own, number: shared_out(jax.random.fold_in(splits[2], 2), own, number, TOK_DEV, EXPERTS, TOP, CAP, 1))(routes_keys, routes_turns).reshape((TOKENS, TOP))
    gates = jnp.clip(0.099609375 + 0.9003906 * jax.random.uniform(splits[3], (TOKENS, TOP), jnp.float32) ** steps_of(splits[3], (TOKENS, TOP), ((0, 256),), -0.2, 0.2), 0.099609375, 1.0).astype(jnp.bfloat16)
    w_gate = noise(splits[4], (EXPERTS, D, FF), D ** -0.5, 0.125, ((0, 64), (2, 4)))
    w_up = noise(splits[5], (EXPERTS, D, FF), D ** -0.5, 0.125, ((0, 64), (2, 4)))
    w_down = noise(splits[6], (EXPERTS, FF, D), FF ** -0.5, 0.15625, ((0, 64), (1, 4)))
    return dict(tokens=tokens, out_grad=out_grad, routes=routes, gates=gates, w_gate=w_gate, w_up=w_up, w_down=w_down)


def reference(tokens, out_grad, routes, gates, w_gate, w_up, w_down):
    devices_all = N_DP * N_EXPERT * N_TENSOR
    assign = TOK_DEV * TOP
    picks = routes.reshape(devices_all, assign)
    onehot = (picks[:, :, None] == jnp.arange(EXPERTS, dtype=jnp.int32)).astype(jnp.int32)
    ranks = jnp.sum(onehot * (jnp.cumsum(onehot, axis=1) - 1), axis=2).astype(jnp.int32)
    device_ids = jnp.arange(devices_all, dtype=jnp.int32)[:, None]
    positions = (picks * devices_all + device_ids) * CAP + ranks
    total_assign = devices_all * assign
    idents = jnp.arange(total_assign, dtype=jnp.int32)
    table = jnp.full((EXPERTS * devices_all * CAP,), total_assign, jnp.int32)
    table = table.at[positions.reshape(-1)].set(idents).reshape(EXPERTS, devices_all * CAP)
    tokens_pad = jnp.concatenate([tokens, jnp.zeros((1, D), tokens.dtype)], axis=0)
    grads_pad = jnp.concatenate([out_grad, jnp.zeros((1, D), out_grad.dtype)], axis=0)
    gates_pad = jnp.concatenate([gates.reshape(-1).astype(jnp.float32), jnp.zeros((1,), jnp.float32)])

    def expert_step(carry, inputs):
        dx_acc, dg_acc = carry
        assign_ids, gate_w, up_w, down_w = inputs
        token_ids = assign_ids // TOP
        rows_x = tokens_pad[token_ids]
        rows_dy = grads_pad[token_ids]
        rows_g = gates_pad[assign_ids]
        pre_gate = jnp.dot(rows_x, gate_w, preferred_element_type=jnp.float32)
        pre_up = jnp.dot(rows_x, up_w, preferred_element_type=jnp.float32)
        back_h = jnp.dot(rows_dy, down_w.T, preferred_element_type=jnp.float32)
        sig = jax.nn.sigmoid(pre_gate)
        act = pre_gate * sig
        hidden = act * pre_up
        scaled = rows_g[:, None] * back_h
        grad_pre_gate = (scaled * pre_up * sig * (1.0 + pre_gate * (1.0 - sig))).astype(jnp.bfloat16)
        grad_pre_up = (scaled * act).astype(jnp.bfloat16)
        rows_out = (jnp.dot(grad_pre_gate, gate_w.T, preferred_element_type=jnp.float32)
                    + jnp.dot(grad_pre_up, up_w.T, preferred_element_type=jnp.float32)).astype(jnp.bfloat16)
        dx_acc = dx_acc.at[token_ids].add(rows_out.astype(jnp.float32))
        dg_acc = dg_acc.at[assign_ids].set(jnp.sum(hidden * back_h, axis=1))
        weighted = (rows_g[:, None] * rows_dy.astype(jnp.float32)).astype(jnp.bfloat16)
        total = jnp.dot(hidden.astype(jnp.bfloat16).T, weighted, preferred_element_type=jnp.float32)
        return (dx_acc, dg_acc), total

    start = (jnp.zeros((TOKENS + 1, D), jnp.float32), jnp.zeros((total_assign + 1,), jnp.float32))
    (dx_acc, dg_acc), grad_down = lax.scan(expert_step, start, (table, w_gate, w_up, w_down))
    grad_tokens = dx_acc[:TOKENS].astype(jnp.bfloat16)
    grad_gate = dg_acc[:total_assign].reshape(TOKENS, TOP).astype(jnp.bfloat16)
    return grad_tokens, grad_gate, grad_down
```

```python
import dataclasses
import functools

import jax
import jax.numpy as jnp
from jax import lax
from jax.experimental import pallas as pl
from jax.experimental.pallas import tpu as pltpu
from jax.sharding import PartitionSpec as P

MESH = pl.DeviceIdType.MESH
F32 = jnp.float32
BF16 = jnp.bfloat16
LANES = 128
CW = 3 * LANES


@dataclasses.dataclass(frozen=True)
class Sizes:
    n_dp: int
    n_x: int
    tok: int
    top: int
    cap: int
    width: int
    ff: int

    @property
    def rows(self):
        return self.n_dp * self.n_x * self.cap

    @property
    def mix(self):
        return self.width // CW

    @property
    def fwd(self):
        return 2 * self.mix + 1

    @property
    def ret(self):
        return self.mix + 1


def dot_nn(a, b):
    return lax.dot_general(a, b, (((1,), (0,)), ((), ())), preferred_element_type=F32)


def dot_nt(a, b):
    return lax.dot_general(a, b, (((1,), (1,)), ((), ())), preferred_element_type=F32)


def onehot(cond):
    return jnp.where(cond, 1.0, 0.0).astype(BF16)


def log2(n):
    assert n & (n - 1) == 0
    return n.bit_length() - 1


def kernel(
    z, routes_ref, gates_ref, tok_ref, dy_ref, wg_hbm, wu_hbm, wd_hbm,
    out_tok, out_gate, out_down,
    xc, sel, rx, sd, g, wg, wu, wd0, wd, pg, pu, hf, ht, bh, gt, gg, gu, gp, mats, pt,
    os_, ora, orb, am, ap, arp, arm, rd, rb, sx, hb,
    w_sem, xs, xr, ds_, dr, ys, yra, yrb, yrc, yrd,
    os_s, ora_r, orb_r, a_s, arp_r, arm_r, rd_s, rb_r, sx_s, hb_r,
):
    dp = lax.axis_index("dp")
    x = lax.axis_index("expert")
    y = lax.axis_index("tensor")
    rows, cap, n_dp, n_x, mix = z.rows, z.cap, z.n_dp, z.n_x, z.mix
    half = rows // 2
    xb, db = n_dp * cap, n_x * cap
    up, down, far = lax.rem(y + 1, 4), lax.rem(y + 3, 4), lax.rem(y + 2, 4)
    dev_up, dev_down = (dp, x, up), (dp, x, down)

    def wcopy(i):
        if i == 0:
            return pltpu.make_async_copy(wg_hbm, wg.at[pl.ds(0, z.width)], w_sem.at[0])
        if i == 1:
            return pltpu.make_async_copy(wu_hbm, wu.at[pl.ds(0, z.width)], w_sem.at[1])
        if i == 2:
            return pltpu.make_async_copy(wd_hbm.at[:, pl.ds(0, LANES)], wd0, w_sem.at[2])
        j = i - 3
        return pltpu.make_async_copy(
            wd_hbm.at[:, pl.ds(LANES + j * CW, CW)], wd.at[j], w_sem.at[i]
        )

    for i in range(3 + mix):
        wcopy(i).start()

    barrier = pltpu.get_barrier_semaphore()

    def greet_dp(j, c):
        pl.semaphore_signal(
            barrier, inc=1, device_id=(lax.rem(dp + j, n_dp), x, y), device_id_type=MESH
        )
        return c

    def greet_x(j, c):
        pl.semaphore_signal(
            barrier, inc=1, device_id=(dp, lax.rem(x + j, n_x), y), device_id_type=MESH
        )
        return c

    lax.fori_loop(1, n_dp, greet_dp, 0)
    lax.fori_loop(1, n_x, greet_x, 0)
    pl.semaphore_signal(barrier, inc=1, device_id=dev_up, device_id_type=MESH)
    pl.semaphore_signal(barrier, inc=1, device_id=dev_down, device_id_type=MESH)

    slot = lax.broadcasted_iota(jnp.int32, (z.tok, rows), 1)
    s_x = slot >> log2(xb)
    s_dp = (slot & (xb - 1)) >> log2(cap)
    s_rank = slot & (cap - 1)
    s_e = s_dp * n_x + s_x
    named = jnp.zeros((z.tok, rows), F32)
    gate = jnp.zeros((z.tok, rows), F32)
    for k in range(z.top):
        hit = routes_ref[:, k : k + 1] == s_e
        named = jnp.where(hit, 1.0, named)
        gate = jnp.where(hit, gates_ref[:, k : k + 1].astype(F32), gate)
    t_row = lax.broadcasted_iota(jnp.int32, (z.tok, z.tok), 0)
    t_col = lax.broadcasted_iota(jnp.int32, (z.tok, z.tok), 1)
    rank = dot_nn(onehot(t_col < t_row), named.astype(BF16))
    picked = jnp.where(rank == s_rank.astype(F32), named, 0.0)
    pt[...] = picked.astype(BF16)
    i_row = lax.broadcasted_iota(jnp.int32, (rows, rows), 0)
    i_col = lax.broadcasted_iota(jnp.int32, (rows, rows), 1)
    eye = onehot(i_row == i_col)
    place = dot_nt(eye, picked.astype(BF16)).astype(BF16)
    place_gate = dot_nt(eye, (picked * gate).astype(BF16)).astype(BF16)
    def reordered(i):
        return (
            ((i & (db - 1)) >> log2(cap)) * xb + (i >> log2(db)) * cap + (i & (cap - 1))
        )

    mats[0] = onehot(i_col == reordered(i_row))
    mats[1] = onehot(i_row == reordered(i_col))

    for q in range(mix):
        xc[q] = tok_ref[:, q * CW : (q + 1) * CW]
        xc[mix + 1 + q] = dy_ref[:, LANES + q * CW : LANES + (q + 1) * CW]
    xc[mix, :, 0:LANES] = tok_ref[:, mix * CW :]
    xc[mix, :, LANES : 2 * LANES] = jnp.zeros((z.tok, LANES), BF16)
    xc[mix, :, 2 * LANES :] = dy_ref[:, 0:LANES]

    def choose(q, c):
        sel[q] = dot_nn(place, xc[q]).astype(BF16)
        return c

    lax.fori_loop(0, z.fwd, choose, 0)
    sel[mix, :, LANES : 2 * LANES] = dot_nn(
        place_gate, jnp.ones((z.tok, LANES), BF16)
    ).astype(BF16)

    def clear(o, c):
        pg[o] = jnp.zeros((rows, z.ff), F32)
        pu[o] = jnp.zeros((rows, z.ff), F32)
        return c

    lax.fori_loop(0, 4, clear, 0)
    wg[pl.ds(z.width, 2 * LANES)] = jnp.zeros((2 * LANES, z.ff), BF16)
    wu[pl.ds(z.width, 2 * LANES)] = jnp.zeros((2 * LANES, z.ff), BF16)

    pl.semaphore_wait(barrier, n_dp - 1 + n_x - 1 + 2)

    def remote(src, dst, send, recv, dev):
        return pltpu.make_async_remote_copy(
            src_ref=src, dst_ref=dst, send_sem=send, recv_sem=recv,
            device_id=dev, device_id_type=MESH,
        )

    def got(region, sem):
        remote(region, region, sem, sem, dev_up).wait_recv()

    def left(region, sem):
        remote(region, region, sem, sem, dev_up).wait_send()

    def f0(q):
        rx[q, pl.ds(pl.multiple_of(x * xb, 16), xb)] = sel[q, pl.ds(pl.multiple_of(x * xb, 16), xb)]

        def send(j, c):
            to = lax.rem(x + j, n_x)
            remote(
                sel.at[q, pl.ds(pl.multiple_of(to * xb, 16), xb)],
                rx.at[q, pl.ds(pl.multiple_of(x * xb, 16), xb)],
                xs.at[q], xr.at[q], (dp, to, y),
            ).start()
            return c

        lax.fori_loop(1, n_x, send, 0)

    def f1(q):
        got(rx.at[q, pl.ds(0, rows - xb)], xr.at[q])
        sd[q] = dot_nn(mats[0], rx[q]).astype(BF16)
        mine = pl.ds(pl.multiple_of(dp * db, 16), db)

        def send(j, c):
            to = lax.rem(dp + j, n_dp)
            remote(
                sd.at[q, pl.ds(pl.multiple_of(to * db, 16), db)],
                g.at[q, y, mine],
                ds_.at[q], dr.at[q], (to, x, y),
            ).start()
            return c

        lax.fori_loop(1, n_dp, send, 0)
        g[q, y, mine] = sd[q, mine]

    def f2(q):
        got(g.at[q, y, pl.ds(0, rows - db)], dr.at[q])
        remote(g.at[q, y], g.at[q, y], ys.at[q], yra.at[q], dev_up).start()
        remote(g.at[q, y], g.at[q, y], ys.at[q], yrb.at[q], dev_down).start()

    def f3(q):
        got(g.at[q, down], yra.at[q])
        first = g.at[q, down, pl.ds(0, half)]
        remote(first, first, ys.at[q], yrc.at[q], dev_up).start()
        got(g.at[q, up], yrb.at[q])
        second = g.at[q, up, pl.ds(half, half)]
        remote(second, second, ys.at[q], yrd.at[q], dev_down).start()

    def f4(q):
        got(g.at[q, far, pl.ds(0, half)], yrc.at[q])
        got(g.at[q, far, pl.ds(half, half)], yrd.at[q])

        @pl.when(q < mix)
        def _():
            part = pl.ds(pl.multiple_of(q * CW, LANES), CW)

            def one(o, c):
                pg[o] += dot_nn(g[q, o], wg[part])
                pu[o] += dot_nn(g[q, o], wu[part])
                return c

            lax.fori_loop(0, 4, one, 0)

        @pl.when(q == mix)
        def _():
            def one(o, down_acc):
                xe = g[q, o, :, 0:LANES]
                tail = pl.ds(mix * CW, LANES)
                pre_gate = pg[o] + dot_nn(xe, wg[tail])
                pre_up = pu[o] + dot_nn(xe, wu[tail])
                sig = 1.0 / (1.0 + jnp.exp(-pre_gate))
                act = pre_gate * sig
                hidden = act * pre_up
                pg[o] = act
                pu[o] = pre_up * sig * (1.0 + pre_gate * (1.0 - sig))
                hf[o] = hidden
                r = lax.broadcasted_iota(jnp.int32, (z.ff, z.ff), 0)
                c = lax.broadcasted_iota(jnp.int32, (z.ff, z.ff), 1)
                ht[o] = dot_nt(onehot(r == c), hidden.astype(BF16)).astype(BF16)
                gt[o] = g[q, o, :, LANES : 2 * LANES].astype(F32)
                dye = g[q, o, :, 2 * LANES : 3 * LANES]
                bh[o] = dot_nt(dye, wd0[...])
                weighted = (gt[o] * dye.astype(F32)).astype(BF16)
                return down_acc + dot_nn(ht[o], weighted)

            out_down[:, 0:LANES] = lax.fori_loop(0, 4, one, jnp.zeros((z.ff, LANES), F32))

        @pl.when(q > mix)
        def _():
            j = q - mix - 1
            cols = pl.ds(pl.multiple_of(LANES + j * CW, LANES), CW)
            out_down[:, cols] = jnp.zeros((z.ff, CW), F32)

            def one(o, c):
                dye = g[q, o]
                bh[o] += dot_nt(dye, wd[j])
                scale = jnp.concatenate([gt[o]] * 3, axis=1)
                weighted = (scale * dye.astype(F32)).astype(BF16)
                out_down[:, cols] += dot_nn(ht[o], weighted)
                return c

            lax.fori_loop(0, 4, one, 0)

    def at(t, n, do):
        pl.when(jnp.logical_and(t >= 0, t < n))(functools.partial(do, t))

    for i in range(3 + mix):
        wcopy(i).wait()

    def tick_out(t, c):
        at(t - 2, z.fwd, f2)
        at(t - 3, z.fwd, f3)
        at(t - 1, z.fwd, f1)
        at(t, z.fwd, f0)
        at(t - 4, z.fwd, f4)
        return c

    lax.fori_loop(0, z.fwd + 4, tick_out, 0)

    def middle(o, c):
        back_h = bh[o]
        scaled = gt[o][:, 0:1] * back_h
        gg[o] = (scaled * pu[o]).astype(BF16)
        gu[o] = (scaled * pg[o]).astype(BF16)
        gp[o] = jnp.broadcast_to(
            jnp.sum(hf[o] * back_h, axis=1, keepdims=True), (rows, LANES)
        )
        return c

    lax.fori_loop(0, 4, middle, 0)

    def partial_rows(o, r):
        part = pl.ds(pl.multiple_of(r * CW, LANES), CW)
        total = dot_nt(gg[o], wg[part]) + dot_nt(gu[o], wu[part])
        lane = lax.broadcasted_iota(jnp.int32, (rows, CW), 1)
        at_gate = jnp.logical_and(lane >= LANES, lane < 2 * LANES)
        extra = jnp.where(at_gate, gp[o][:, 0:1], 0.0)
        return total + jnp.where(r == mix, 1.0, 0.0) * extra

    lo, hi = pl.ds(0, half), pl.ds(half, half)

    def r0(r):
        os_[r] = partial_rows(far, r).astype(BF16)
        remote(os_.at[r, lo], ora.at[r], os_s.at[r], ora_r.at[r], dev_down).start()
        remote(os_.at[r, hi], orb.at[r], os_s.at[r], orb_r.at[r], dev_up).start()

    def r1(r):
        mine = partial_rows(down, r)
        got(ora.at[r], ora_r.at[r])
        am[r, lo] = (mine[0:half] + ora[r].astype(F32)).astype(BF16)
        am[r, hi] = mine[half:].astype(BF16)
        remote(am.at[r], arp.at[r], a_s.at[r], arp_r.at[r], dev_down).start()
        mine = partial_rows(up, r)
        got(orb.at[r], orb_r.at[r])
        ap[r, lo] = mine[0:half].astype(BF16)
        ap[r, hi] = (mine[half:] + orb[r].astype(F32)).astype(BF16)
        remote(ap.at[r], arm.at[r], a_s.at[r], arm_r.at[r], dev_up).start()

    def r2(r):
        mine = partial_rows(y, r)
        got(arp.at[r], arp_r.at[r])
        got(arm.at[r], arm_r.at[r])
        rd[r] = (mine + arp[r].astype(F32) + arm[r].astype(F32)).astype(BF16)
        own = pl.ds(pl.multiple_of(dp * db, 16), db)

        def send(j, c):
            to = lax.rem(dp + j, n_dp)
            remote(
                rd.at[r, pl.ds(pl.multiple_of(to * db, 16), db)], rb.at[r, own],
                rd_s.at[r], rb_r.at[r], (to, x, y),
            ).start()
            return c

        lax.fori_loop(1, n_dp, send, 0)
        rb[r, own] = rd[r, own]

    def r3(r):
        got(rb.at[r, pl.ds(0, rows - db)], rb_r.at[r])
        sx[r] = dot_nn(mats[1], rb[r]).astype(BF16)
        own = pl.ds(pl.multiple_of(x * xb, 16), xb)

        def send(j, c):
            to = lax.rem(x + j, n_x)
            remote(
                sx.at[r, pl.ds(pl.multiple_of(to * xb, 16), xb)], hb.at[r, own],
                sx_s.at[r], hb_r.at[r], (dp, to, y),
            ).start()
            return c

        lax.fori_loop(1, n_x, send, 0)
        hb[r, own] = sx[r, own]

    def r4(r):
        got(hb.at[r, pl.ds(0, rows - xb)], hb_r.at[r])

        @pl.when(r < mix)
        def _():
            cols = pl.ds(pl.multiple_of(r * CW, LANES), CW)
            out_tok[:, cols] = dot_nn(pt[...], hb[r]).astype(BF16)

        @pl.when(r == mix)
        def _():
            out_tok[:, mix * CW :] = dot_nn(pt[...], hb[r, :, 0:LANES]).astype(BF16)
            row = lax.broadcasted_iota(jnp.int32, (rows, LANES), 0)
            lane = lax.broadcasted_iota(jnp.int32, (rows, LANES), 1)
            e = ((row & (xb - 1)) >> log2(cap)) * n_x + (row >> log2(xb))
            vals = jnp.where(e == lane, hb[r, :, LANES : 2 * LANES].astype(F32), 0.0)
            by_expert = dot_nn(pt[...], vals.astype(BF16))
            lane_t = lax.broadcasted_iota(jnp.int32, (z.tok, LANES), 1)
            for k in range(z.top):
                hit = routes_ref[:, k : k + 1] == lane_t
                out_gate[:, k : k + 1] = jnp.sum(
                    jnp.where(hit, by_expert, 0.0), axis=1, keepdims=True
                ).astype(BF16)

    def tick_back(t, c):
        at(t, z.ret, r0)
        at(t - 1, z.ret, r1)
        at(t - 2, z.ret, r2)
        at(t - 3, z.ret, r3)
        at(t - 4, z.ret, r4)
        return c

    lax.fori_loop(0, z.ret + 4, tick_back, 0)

    def drain_out(q, c):
        left(sel.at[q, pl.ds(0, rows - xb)], xs.at[q])
        left(sd.at[q, pl.ds(0, rows - db)], ds_.at[q])
        left(g.at[q, pl.ds(0, 3)], ys.at[q])
        return c

    def drain_back(r, c):
        left(os_.at[r], os_s.at[r])
        left(g.at[r, pl.ds(0, 2)], a_s.at[r])
        left(rd.at[r, pl.ds(0, rows - db)], rd_s.at[r])
        left(sx.at[r, pl.ds(0, rows - xb)], sx_s.at[r])
        return c

    lax.fori_loop(0, z.fwd, drain_out, 0)
    lax.fori_loop(0, z.ret, drain_back, 0)


def body(cap, tokens, out_grad, routes, gates, w_gate, w_up, w_down):
    z = Sizes(
        n_dp=lax.axis_size("dp"), n_x=lax.axis_size("expert"), tok=tokens.shape[0],
        top=routes.shape[1], cap=cap, width=tokens.shape[1], ff=w_gate.shape[2],
    )
    assert lax.axis_size("tensor") == 4 and z.width % CW == LANES
    rows, half, fwd, ret, mix = z.rows, z.rows // 2, z.fwd, z.ret, z.mix
    vm = pltpu.VMEM
    sem = pltpu.SemaphoreType.DMA
    scratch = [
        vm((fwd, z.tok, CW), BF16),
        vm((fwd, rows, CW), BF16),
        vm((fwd, rows, CW), BF16),
        vm((fwd, rows, CW), BF16),
        vm((fwd, 4, rows, CW), BF16),
        vm((z.width + 2 * LANES, z.ff), BF16),
        vm((z.width + 2 * LANES, z.ff), BF16),
        vm((z.ff, LANES), BF16),
        vm((mix, z.ff, CW), BF16),
        vm((4, rows, z.ff), F32),
        vm((4, rows, z.ff), F32),
        vm((4, rows, z.ff), F32),
        vm((4, z.ff, rows), BF16),
        vm((4, rows, z.ff), F32),
        vm((4, rows, LANES), F32),
        vm((4, rows, z.ff), BF16),
        vm((4, rows, z.ff), BF16),
        vm((4, rows, LANES), F32),
        vm((2, rows, rows), BF16),
        vm((z.tok, rows), BF16),
        vm((ret, rows, CW), BF16),
        vm((ret, half, CW), BF16),
        vm((ret, half, CW), BF16),
        vm((ret, rows, CW), BF16),
        vm((ret, rows, CW), BF16),
        vm((ret, rows, CW), BF16),
        vm((ret, rows, CW), BF16),
        vm((ret, rows, CW), BF16),
        vm((ret, rows, CW), BF16),
        vm((ret, rows, CW), BF16),
        vm((ret, rows, CW), BF16),
        sem((3 + mix,)),
    ] + [sem((fwd,))] * 9 + [sem((ret,))] * 10
    vmem = pl.BlockSpec(memory_space=pltpu.VMEM)
    hbm = pl.BlockSpec(memory_space=pl.ANY)
    grad_tokens, grad_gate, grad_down = pl.pallas_call(
        functools.partial(kernel, z),
        out_shape=(
            jax.ShapeDtypeStruct((z.tok, z.width), BF16),
            jax.ShapeDtypeStruct((z.tok, z.top), BF16),
            jax.ShapeDtypeStruct((z.ff, z.width), F32),
        ),
        in_specs=[vmem] * 4 + [hbm] * 3,
        out_specs=(vmem, vmem, vmem),
        scratch_shapes=scratch,
        compiler_params=pltpu.CompilerParams(
            collective_id=0, has_side_effects=True, vmem_limit_bytes=60 * 1024 * 1024
        ),
    )(routes, gates, tokens, out_grad, w_gate[0], w_up[0], w_down[0])
    return grad_tokens, grad_gate, grad_down[None]


def solution(mesh, cap=4):
    tokens = P(("dp", "expert", "tensor"), None)
    return jax.shard_map(
        functools.partial(body, cap),
        mesh=mesh,
        in_specs=(
            tokens, tokens, tokens, tokens,
            P(("dp", "expert"), None, "tensor"),
            P(("dp", "expert"), None, "tensor"),
            P(("dp", "expert"), "tensor", None),
        ),
        out_specs=(tokens, tokens, P(("dp", "expert"), "tensor", None)),
        check_vma=False,
    )
```

```python
import dataclasses
import functools

import jax
import jax.numpy as jnp
from jax import lax
from jax.experimental import pallas as pl
from jax.experimental.pallas import tpu as pltpu
from jax.sharding import PartitionSpec as P

MESH = pl.DeviceIdType.MESH
F32 = jnp.float32
BF16 = jnp.bfloat16
LANES = 128
CW = 3 * LANES


@dataclasses.dataclass(frozen=True)
class Sizes:
    n_dp: int
    n_x: int
    tok: int
    top: int
    cap: int
    width: int
    ff: int

    @property
    def rows(self):
        return self.n_dp * self.n_x * self.cap

    @property
    def mix(self):
        return self.width // CW

    @property
    def fwd(self):
        return 2 * self.mix + 1

    @property
    def ret(self):
        return self.mix + 1


def dot_nn(a, b):
    return lax.dot_general(a, b, (((1,), (0,)), ((), ())), preferred_element_type=F32)


def dot_nt(a, b):
    return lax.dot_general(a, b, (((1,), (1,)), ((), ())), preferred_element_type=F32)


def onehot(cond):
    return jnp.where(cond, 1.0, 0.0).astype(BF16)


def log2(n):
    assert n & (n - 1) == 0
    return n.bit_length() - 1


def kernel(
    z, routes_ref, gates_ref, tok_ref, dy_ref, wg_hbm, wu_hbm, wd_hbm,
    out_tok, out_gate, down_hbm,
    out_down, place_ref, gate_slots_ref, xc, sel, rx, sd, g, wg, wu, wd0, wd, pg, pu, hf, ht, bh, gt, gg, gu, gp, mats, pt,
    os_, ora, orb, am, ap, arp, arm, rd, rb, sx, hb,
    w_sem, d_sem, xs, xr, ds_, dr, ys, yra, yrb, yrc, yrd,
    os_s, ora_r, orb_r, a_s, arp_r, arm_r, rd_s, rb_r, sx_s, hb_r,
):
    dp = lax.axis_index("dp")
    x = lax.axis_index("expert")
    y = lax.axis_index("tensor")
    rows, cap, n_dp, n_x, mix = z.rows, z.cap, z.n_dp, z.n_x, z.mix
    half = rows // 2
    xb, db = n_dp * cap, n_x * cap
    up, down, far = lax.rem(y + 1, 4), lax.rem(y + 3, 4), lax.rem(y + 2, 4)
    dev_up, dev_down = (dp, x, up), (dp, x, down)

    def wcopy(i):
        if i == 0:
            return pltpu.make_async_copy(wg_hbm, wg, w_sem.at[0])
        if i == 1:
            return pltpu.make_async_copy(wu_hbm, wu, w_sem.at[1])
        if i == 2:
            return pltpu.make_async_copy(wd_hbm.at[:, pl.ds(0, LANES)], wd0, w_sem.at[2])
        j = i - 3
        return pltpu.make_async_copy(
            wd_hbm.at[:, pl.ds(LANES + j * CW, CW)], wd.at[j], w_sem.at[i]
        )

    def down_copy(j):
        if isinstance(j, int) and j == mix:
            cols = pl.ds(0, LANES)
        else:
            cols = pl.ds(pl.multiple_of(LANES + j * CW, LANES), CW)
        return pltpu.make_async_copy(out_down.at[:, cols], down_hbm.at[:, cols], d_sem.at[j])

    for i in range(3 + mix):
        wcopy(i).start()

    barrier = pltpu.get_barrier_semaphore()

    def greet_dp(j, c):
        pl.semaphore_signal(
            barrier, inc=1, device_id=(lax.rem(dp + j, n_dp), x, y), device_id_type=MESH
        )
        return c

    def greet_x(j, c):
        pl.semaphore_signal(
            barrier, inc=1, device_id=(dp, lax.rem(x + j, n_x), y), device_id_type=MESH
        )
        return c

    lax.fori_loop(1, n_dp, greet_dp, 0)
    lax.fori_loop(1, n_x, greet_x, 0)
    pl.semaphore_signal(barrier, inc=1, device_id=dev_up, device_id_type=MESH)
    pl.semaphore_signal(barrier, inc=1, device_id=dev_down, device_id_type=MESH)

    slot = lax.broadcasted_iota(jnp.int32, (rows, z.tok), 0)
    s_x = slot >> log2(xb)
    s_dp = (slot & (xb - 1)) >> log2(cap)
    s_rank = slot & (cap - 1)
    s_e = s_dp * n_x + s_x
    named = jnp.zeros((rows, z.tok), F32)
    gate = jnp.zeros((rows, z.tok), F32)
    for k in range(z.top):
        hit = routes_ref[k : k + 1, :] == s_e
        named = jnp.where(hit, 1.0, named)
        gate = jnp.where(hit, gates_ref[k : k + 1, :].astype(F32), gate)
    t_row = lax.broadcasted_iota(jnp.int32, (z.tok, z.tok), 0)
    t_col = lax.broadcasted_iota(jnp.int32, (z.tok, z.tok), 1)
    rank = dot_nn(named.astype(BF16), onehot(t_row < t_col))
    picked = jnp.where(rank == s_rank.astype(F32), named, 0.0)
    place_ref[...] = picked.astype(BF16)
    gate_slots_ref[...] = dot_nn(
        (picked * gate).astype(BF16), jnp.ones((z.tok, LANES), BF16)
    ).astype(BF16)
    for q in range(mix):
        xc[q] = tok_ref[:, q * CW : (q + 1) * CW]
        xc[mix + 1 + q] = dy_ref[:, LANES + q * CW : LANES + (q + 1) * CW]
    xc[mix, :, 0:LANES] = tok_ref[:, mix * CW :]
    xc[mix, :, LANES : 2 * LANES] = jnp.zeros((z.tok, LANES), BF16)
    xc[mix, :, 2 * LANES :] = dy_ref[:, 0:LANES]

    def choose(q):
        sel[q] = dot_nn(place_ref[...], xc[q]).astype(BF16)

    for q in range(min(2, z.fwd)):
        choose(q)

    pl.semaphore_wait(barrier, n_dp - 1 + n_x - 1 + 2)

    def remote(src, dst, send, recv, dev):
        return pltpu.make_async_remote_copy(
            src_ref=src, dst_ref=dst, send_sem=send, recv_sem=recv,
            device_id=dev, device_id_type=MESH,
        )

    def got(region, sem):
        remote(region, region, sem, sem, dev_up).wait_recv()

    def left(region, sem):
        remote(region, region, sem, sem, dev_up).wait_send()

    def f0(q):
        @pl.when(q >= 2)
        def _():
            choose(q)

        @pl.when(q == mix)
        def _():
            sel[q, :, LANES : 2 * LANES] = gate_slots_ref[...]

        rx[q, pl.ds(pl.multiple_of(x * xb, 16), xb)] = sel[q, pl.ds(pl.multiple_of(x * xb, 16), xb)]

        def send(j, c):
            to = lax.rem(x + j, n_x)
            remote(
                sel.at[q, pl.ds(pl.multiple_of(to * xb, 16), xb)],
                rx.at[q, pl.ds(pl.multiple_of(x * xb, 16), xb)],
                xs.at[q], xr.at[q], (dp, to, y),
            ).start()
            return c

        lax.fori_loop(1, n_x, send, 0)

    def f1(q):
        got(rx.at[q, pl.ds(0, rows - xb)], xr.at[q])
        sd[q] = dot_nn(mats[0], rx[q]).astype(BF16)
        mine = pl.ds(pl.multiple_of(dp * db, 16), db)

        def send(j, c):
            to = lax.rem(dp + j, n_dp)
            remote(
                sd.at[q, pl.ds(pl.multiple_of(to * db, 16), db)],
                g.at[q, y, mine],
                ds_.at[q], dr.at[q], (to, x, y),
            ).start()
            return c

        lax.fori_loop(1, n_dp, send, 0)
        g[q, y, mine] = sd[q, mine]

    def f2(q):
        got(g.at[q, y, pl.ds(0, rows - db)], dr.at[q])
        remote(g.at[q, y], g.at[q, y], ys.at[q], yra.at[q], dev_up).start()
        remote(g.at[q, y], g.at[q, y], ys.at[q], yrb.at[q], dev_down).start()

    def f3(q):
        got(g.at[q, down], yra.at[q])
        first = g.at[q, down, pl.ds(0, half)]
        remote(first, first, ys.at[q], yrc.at[q], dev_up).start()
        got(g.at[q, up], yrb.at[q])
        second = g.at[q, up, pl.ds(half, half)]
        remote(second, second, ys.at[q], yrd.at[q], dev_down).start()

    def f4(q):
        got(g.at[q, far, pl.ds(0, half)], yrc.at[q])
        got(g.at[q, far, pl.ds(half, half)], yrd.at[q])

        @pl.when(q == 0)
        def _():
            def one(o, c):
                pg[o] = dot_nt(g[q, o], wg[:, 0:CW])
                pu[o] = dot_nt(g[q, o], wu[:, 0:CW])
                return c

            lax.fori_loop(0, 4, one, 0)

        @pl.when(jnp.logical_and(q > 0, q < mix))
        def _():
            part = pl.ds(pl.multiple_of(q * CW, LANES), CW)

            def one(o, c):
                pg[o] += dot_nt(g[q, o], wg[:, part])
                pu[o] += dot_nt(g[q, o], wu[:, part])
                return c

            lax.fori_loop(0, 4, one, 0)

        @pl.when(q == mix)
        def _():
            def one(o, down_acc):
                xe = g[q, o, :, 0:LANES]
                tail = pl.ds(mix * CW, LANES)
                pre_gate = pg[o] + dot_nt(xe, wg[:, tail])
                pre_up = pu[o] + dot_nt(xe, wu[:, tail])
                sig = 1.0 / (1.0 + jnp.exp(-pre_gate))
                act = pre_gate * sig
                hidden = act * pre_up
                pg[o] = act
                pu[o] = pre_up * sig * (1.0 + pre_gate * (1.0 - sig))
                hf[o] = hidden
                r = lax.broadcasted_iota(jnp.int32, (z.ff, z.ff), 0)
                c = lax.broadcasted_iota(jnp.int32, (z.ff, z.ff), 1)
                ht[o] = dot_nt(onehot(r == c), hidden.astype(BF16)).astype(BF16)
                gt[o] = g[q, o, :, LANES : 2 * LANES].astype(F32)
                dye = g[q, o, :, 2 * LANES : 3 * LANES]
                bh[o] = dot_nt(dye, wd0[...])
                weighted = (gt[o] * dye.astype(F32)).astype(BF16)
                return down_acc + dot_nn(ht[o], weighted)

            out_down[:, 0:LANES] = lax.fori_loop(0, 4, one, jnp.zeros((z.ff, LANES), F32))
            down_copy(mix).start()

        @pl.when(q > mix)
        def _():
            j = q - mix - 1

            def one(o, c):
                bh[o] += dot_nt(g[q, o], wd[j])
                return c

            lax.fori_loop(0, 4, one, 0)

        pl.when(jnp.logical_and(q > mix, q < z.fwd - 1))(functools.partial(grad_down, q))

    def grad_down(q):
        j = q - mix - 1
        cols = pl.ds(pl.multiple_of(LANES + j * CW, LANES), CW)

        def weighted(o):
            scale = jnp.concatenate([gt[o]] * 3, axis=1)
            return (scale * g[q, o].astype(F32)).astype(BF16)

        total = dot_nn(ht[0], weighted(0))
        for o in range(1, 4):
            total += dot_nn(ht[o], weighted(o))
        out_down[:, cols] = total
        down_copy(j).start()

    def at(t, n, do):
        pl.when(jnp.logical_and(t >= 0, t < n))(functools.partial(do, t))

    for q in range(min(3, z.fwd)):
        f0(jnp.int32(q))
    pt[...] = dot_nt(onehot(t_row == t_col), place_ref[...]).astype(BF16)
    i_row = lax.broadcasted_iota(jnp.int32, (rows, rows), 0)
    i_col = lax.broadcasted_iota(jnp.int32, (rows, rows), 1)

    def reordered(i):
        return (
            ((i & (db - 1)) >> log2(cap)) * xb + (i >> log2(db)) * cap + (i & (cap - 1))
        )

    mats[0] = onehot(i_col == reordered(i_row))
    mats[1] = onehot(i_row == reordered(i_col))


    for i in range(3 + mix):
        wcopy(i).wait()

    def tick_out(t, c):
        at(t - 4, z.fwd, f3)
        at(t - 2, z.fwd, f2)
        at(t, z.fwd, f1)
        at(t + 3, z.fwd, f0)
        at(t - 5, z.fwd, f4)
        return c

    lax.fori_loop(0, z.fwd + 5, tick_out, 0)

    def middle(o):
        back_h = bh[o]
        scaled = gt[o][:, 0:1] * back_h
        gg[o] = (scaled * pu[o]).astype(BF16)
        gu[o] = (scaled * pg[o]).astype(BF16)
        gp[o] = jnp.broadcast_to(
            jnp.sum(hf[o] * back_h, axis=1, keepdims=True), (rows, LANES)
        )

    def partial_rows(o, r, w):
        if w == CW:
            part = pl.ds(pl.multiple_of(r * CW, LANES), CW)
            return dot_nn(gg[o], wg[:, part]) + dot_nn(gu[o], wu[:, part])
        tail = pl.ds(mix * CW, LANES)
        total = dot_nn(gg[o], wg[:, tail]) + dot_nn(gu[o], wu[:, tail])
        return jnp.concatenate([total, gp[o]], axis=1)

    lo, hi = pl.ds(0, half), pl.ds(half, half)

    def r0(r, w):
        cs = pl.ds(0, w)
        os_[r, :, cs] = partial_rows(far, r, w).astype(BF16)
        remote(os_.at[r, lo, cs], ora.at[r, :, cs], os_s.at[r], ora_r.at[r], dev_down).start()
        remote(os_.at[r, hi, cs], orb.at[r, :, cs], os_s.at[r], orb_r.at[r], dev_up).start()

    def r1(r, w):
        cs = pl.ds(0, w)
        mine = partial_rows(down, r, w)
        got(ora.at[r, :, cs], ora_r.at[r])
        am[r, lo, cs] = (mine[0:half] + ora[r, :, cs].astype(F32)).astype(BF16)
        am[r, hi, cs] = mine[half:].astype(BF16)
        remote(am.at[r, :, cs], arp.at[r, :, cs], a_s.at[r], arp_r.at[r], dev_down).start()
        mine = partial_rows(up, r, w)
        got(orb.at[r, :, cs], orb_r.at[r])
        ap[r, lo, cs] = mine[0:half].astype(BF16)
        ap[r, hi, cs] = (mine[half:] + orb[r, :, cs].astype(F32)).astype(BF16)
        remote(ap.at[r, :, cs], arm.at[r, :, cs], a_s.at[r], arm_r.at[r], dev_up).start()

    def r2(r, w):
        cs = pl.ds(0, w)
        mine = partial_rows(y, r, w)
        got(arp.at[r, :, cs], arp_r.at[r])
        got(arm.at[r, :, cs], arm_r.at[r])
        rd[r, :, cs] = (
            mine + arp[r, :, cs].astype(F32) + arm[r, :, cs].astype(F32)
        ).astype(BF16)
        own = pl.ds(pl.multiple_of(dp * db, 16), db)

        def send(j, c):
            to = lax.rem(dp + j, n_dp)
            remote(
                rd.at[r, pl.ds(pl.multiple_of(to * db, 16), db), cs], rb.at[r, own, cs],
                rd_s.at[r], rb_r.at[r], (to, x, y),
            ).start()
            return c

        lax.fori_loop(1, n_dp, send, 0)
        rb[r, own, cs] = rd[r, own, cs]

    def r3(r, w):
        cs = pl.ds(0, w)
        got(rb.at[r, pl.ds(0, rows - db), cs], rb_r.at[r])
        sx[r, :, cs] = dot_nn(mats[1], rb[r, :, cs]).astype(BF16)
        own = pl.ds(pl.multiple_of(x * xb, 16), xb)

        def send(j, c):
            to = lax.rem(x + j, n_x)
            remote(
                sx.at[r, pl.ds(pl.multiple_of(to * xb, 16), xb), cs], hb.at[r, own, cs],
                sx_s.at[r], hb_r.at[r], (dp, to, y),
            ).start()
            return c

        lax.fori_loop(1, n_x, send, 0)
        hb[r, own, cs] = sx[r, own, cs]

    def r4(r, w):
        got(hb.at[r, pl.ds(0, rows - xb), pl.ds(0, w)], hb_r.at[r])
        if w == CW:
            cols = pl.ds(pl.multiple_of(r * CW, LANES), CW)
            out_tok[:, cols] = dot_nn(pt[...], hb[r]).astype(BF16)
            return
        out_tok[:, mix * CW :] = dot_nn(pt[...], hb[r, :, 0:LANES]).astype(BF16)
        row = lax.broadcasted_iota(jnp.int32, (rows, LANES), 0)
        lane = lax.broadcasted_iota(jnp.int32, (rows, LANES), 1)
        e = ((row & (xb - 1)) >> log2(cap)) * n_x + (row >> log2(xb))
        vals = jnp.where(e == lane, hb[r, :, LANES : 2 * LANES].astype(F32), 0.0)
        by_expert = dot_nn(pt[...], vals.astype(BF16))
        e_row = lax.broadcasted_iota(jnp.int32, (LANES, LANES), 0)
        e_col = lax.broadcasted_iota(jnp.int32, (LANES, LANES), 1)
        by_expert = dot_nt(onehot(e_row == e_col), by_expert.astype(BF16))
        e_tok = lax.broadcasted_iota(jnp.int32, (LANES, z.tok), 0)
        for k in range(z.top):
            hit = routes_ref[k : k + 1, :] == e_tok
            out_gate[k : k + 1, :] = jnp.sum(
                jnp.where(hit, by_expert, 0.0), axis=0, keepdims=True
            ).astype(BF16)

    def back(t, do):
        pl.when(jnp.logical_and(t >= 0, t < mix))(functools.partial(do, t, CW))
        pl.when(t == mix)(functools.partial(do, t, 2 * LANES))

    def tick_back(t, c):
        back(t - 2, r1)
        back(t, r0)
        back(t - 4, r2)
        back(t - 6, r3)
        back(t - 8, r4)
        return c

    middle(far)
    r0(0, CW)
    for o in (down, up, y):
        middle(o)
    grad_down(z.fwd - 1)
    lax.fori_loop(1, z.ret + 8, tick_back, 0)

    def drain_out(q, c):
        left(sel.at[q, pl.ds(0, rows - xb)], xs.at[q])
        left(sd.at[q, pl.ds(0, rows - db)], ds_.at[q])
        left(g.at[q, pl.ds(0, 3)], ys.at[q])
        return c

    def drain_back(r, w):
        cs = pl.ds(0, w)
        left(os_.at[r, :, cs], os_s.at[r])
        left(g.at[r, pl.ds(0, 2), :, cs], a_s.at[r])
        left(rd.at[r, pl.ds(0, rows - db), cs], rd_s.at[r])
        left(sx.at[r, pl.ds(0, rows - xb), cs], sx_s.at[r])

    lax.fori_loop(0, z.fwd, drain_out, 0)
    for j in range(mix + 1):
        down_copy(j).wait()
    for r in range(mix):
        drain_back(r, CW)
    drain_back(mix, 2 * LANES)


def hand_over(tok_in, gate_in, down_in, tok_out, gate_out, down_out, tok, gate, down, sem):
    parts = [(tok_in, tok, tok_out), (gate_in, gate, gate_out)]
    step = down.shape[0] // 4
    for i in range(4):
        part = pl.ds(i * step, step)
        parts.append((down_in.at[part], down.at[part], down_out.at[part]))
    reads = [
        pltpu.make_async_copy(a, b, sem.at[0, i]) for i, (a, b, _) in enumerate(parts)
    ]
    writes = [
        pltpu.make_async_copy(b, c, sem.at[1, i]) for i, (_, b, c) in enumerate(parts)
    ]
    for read in reads:
        read.start()
    for read, write in zip(reads, writes):
        read.wait()
        write.start()
    for write in writes:
        write.wait()


def body(cap, tokens, out_grad, routes, gates, w_gate, w_up, w_down):
    z = Sizes(
        n_dp=lax.axis_size("dp"), n_x=lax.axis_size("expert"), tok=tokens.shape[0],
        top=routes.shape[1], cap=cap, width=tokens.shape[1], ff=w_gate.shape[2],
    )
    assert lax.axis_size("tensor") == 4 and z.width % CW == LANES
    rows, half, fwd, ret, mix = z.rows, z.rows // 2, z.fwd, z.ret, z.mix
    vm = pltpu.VMEM
    sem = pltpu.SemaphoreType.DMA
    scratch = [
        vm((z.ff, z.width), F32),
        vm((rows, z.tok), BF16),
        vm((rows, LANES), BF16),
        vm((fwd, z.tok, CW), BF16),
        vm((fwd, rows, CW), BF16),
        vm((fwd, rows, CW), BF16),
        vm((fwd, rows, CW), BF16),
        vm((fwd, 4, rows, CW), BF16),
        vm((z.ff, z.width), BF16),
        vm((z.ff, z.width), BF16),
        vm((z.ff, LANES), BF16),
        vm((mix, z.ff, CW), BF16),
        vm((4, rows, z.ff), F32),
        vm((4, rows, z.ff), F32),
        vm((4, rows, z.ff), F32),
        vm((4, z.ff, rows), BF16),
        vm((4, rows, z.ff), F32),
        vm((4, rows, LANES), F32),
        vm((4, rows, z.ff), BF16),
        vm((4, rows, z.ff), BF16),
        vm((4, rows, LANES), F32),
        vm((2, rows, rows), BF16),
        vm((z.tok, rows), BF16),
        vm((ret, rows, CW), BF16),
        vm((ret, half, CW), BF16),
        vm((ret, half, CW), BF16),
        vm((ret, rows, CW), BF16),
        vm((ret, rows, CW), BF16),
        vm((ret, rows, CW), BF16),
        vm((ret, rows, CW), BF16),
        vm((ret, rows, CW), BF16),
        vm((ret, rows, CW), BF16),
        vm((ret, rows, CW), BF16),
        vm((ret, rows, CW), BF16),
        sem((3 + mix,)),
        sem((mix + 1,)),
    ] + [sem((fwd,))] * 9 + [sem((ret,))] * 10
    vmem = pl.BlockSpec(memory_space=pltpu.VMEM)
    hbm = pl.BlockSpec(memory_space=pl.ANY)
    grad_tokens, grad_gate, grad_down = pl.pallas_call(
        functools.partial(kernel, z),
        out_shape=(
            jax.ShapeDtypeStruct((z.tok, z.width), BF16),
            jax.ShapeDtypeStruct((z.top, z.tok), BF16),
            jax.ShapeDtypeStruct((z.ff, z.width), F32),
        ),
        in_specs=[vmem] * 4 + [hbm] * 3,
        out_specs=(vmem, vmem, hbm),
        scratch_shapes=scratch,
        compiler_params=pltpu.CompilerParams(
            collective_id=0, has_side_effects=True, vmem_limit_bytes=60 * 1024 * 1024
        ),
    )(routes.T, gates.T, tokens, out_grad, w_gate[0].T, w_up[0].T, w_down[0])
    results = (grad_tokens, grad_gate, grad_down)
    grad_tokens, grad_gate, grad_down = pl.pallas_call(
        hand_over,
        out_shape=tuple(jax.ShapeDtypeStruct(r.shape, r.dtype) for r in results),
        in_specs=[hbm] * 3,
        out_specs=(hbm,) * 3,
        scratch_shapes=[vm(r.shape, r.dtype) for r in results] + [sem((2, 6))],
    )(*results)
    return grad_tokens, grad_gate.T, grad_down[None]


def solution(mesh, cap=4):
    tokens = P(("dp", "expert", "tensor"), None)
    return jax.shard_map(
        functools.partial(body, cap),
        mesh=mesh,
        in_specs=(
            tokens, tokens, tokens, tokens,
            P(("dp", "expert"), None, "tensor"),
            P(("dp", "expert"), None, "tensor"),
            P(("dp", "expert"), "tensor", None),
        ),
        out_specs=(tokens, tokens, P(("dp", "expert"), "tensor", None)),
        check_vma=False,
    )
```

```python
import dataclasses
import functools

import jax
import jax.numpy as jnp
from jax import lax
from jax.experimental import pallas as pl
from jax.experimental.pallas import tpu as pltpu
from jax.sharding import PartitionSpec as P

MESH = pl.DeviceIdType.MESH
F32 = jnp.float32
BF16 = jnp.bfloat16
LANES = 128
CW = 2 * LANES
AHEAD = 4


@dataclasses.dataclass(frozen=True)
class Sizes:
    n_dp: int
    n_x: int
    tok: int
    top: int
    cap: int
    width: int
    ff: int

    @property
    def rows(self):
        return self.n_dp * self.n_x * self.cap

    @property
    def mix(self):
        return self.width // CW

    @property
    def fwd(self):
        return 2 * self.mix + 1

    @property
    def ret(self):
        return self.mix + 1


def dot_nn(a, b):
    return lax.dot_general(a, b, (((1,), (0,)), ((), ())), preferred_element_type=F32)


def dot_nt(a, b):
    return lax.dot_general(a, b, (((1,), (1,)), ((), ())), preferred_element_type=F32)


def onehot(cond):
    return jnp.where(cond, 1.0, 0.0).astype(BF16)


def log2(n):
    assert n & (n - 1) == 0
    return n.bit_length() - 1


def kernel(
    z, routes_ref, gates_ref, tok_ref, dy_ref, wg_hbm, wu_hbm, wd_hbm,
    out_tok, out_gate, down_hbm,
    out_down, place_ref, xc, sel, rx, sd, g, wg, wu, wd, pg, pu, hf, ht, bh, gt, gg, gu, gp, mats, pt,
    os_, ora, orb, am, ap, arp, arm, rd, rb, sx, hb,
    w_sem, d_sem, xs, xr, ds_, dr, ys, yra, yrb, yrc, yrd,
    os_s, ora_r, orb_r, a_s, arp_r, arm_r, rd_s, rb_r, sx_s, hb_r,
):
    dp = lax.axis_index("dp")
    x = lax.axis_index("expert")
    y = lax.axis_index("tensor")
    rows, cap, n_dp, n_x, mix = z.rows, z.cap, z.n_dp, z.n_x, z.mix
    half = rows // 2
    xb, db = n_dp * cap, n_x * cap
    up, down, far = lax.rem(y + 1, 4), lax.rem(y + 3, 4), lax.rem(y + 2, 4)
    dev_up, dev_down = (dp, x, up), (dp, x, down)

    def wcopy(i):
        if i == 0:
            return pltpu.make_async_copy(wg_hbm, wg, w_sem.at[0])
        if i == 1:
            return pltpu.make_async_copy(wu_hbm, wu, w_sem.at[1])
        j = i - 2
        return pltpu.make_async_copy(
            wd_hbm.at[:, pl.ds(j * CW, CW)], wd.at[j], w_sem.at[i]
        )

    def down_copy(j):
        cols = pl.ds(pl.multiple_of(j * CW, CW), CW)
        return pltpu.make_async_copy(out_down.at[:, cols], down_hbm.at[:, cols], d_sem.at[j])

    for i in range(2 + mix):
        wcopy(i).start()

    barrier = pltpu.get_barrier_semaphore()

    def greet_dp(j, c):
        pl.semaphore_signal(
            barrier, inc=1, device_id=(lax.rem(dp + j, n_dp), x, y), device_id_type=MESH
        )
        return c

    def greet_x(j, c):
        pl.semaphore_signal(
            barrier, inc=1, device_id=(dp, lax.rem(x + j, n_x), y), device_id_type=MESH
        )
        return c

    lax.fori_loop(1, n_dp, greet_dp, 0)
    lax.fori_loop(1, n_x, greet_x, 0)
    pl.semaphore_signal(barrier, inc=1, device_id=dev_up, device_id_type=MESH)
    pl.semaphore_signal(barrier, inc=1, device_id=dev_down, device_id_type=MESH)

    slot = lax.broadcasted_iota(jnp.int32, (rows, z.tok), 0)
    s_x = slot >> log2(xb)
    s_dp = (slot & (xb - 1)) >> log2(cap)
    s_rank = slot & (cap - 1)
    s_e = s_dp * n_x + s_x
    named = jnp.zeros((rows, z.tok), F32)
    gate = jnp.zeros((rows, z.tok), F32)
    for k in range(z.top):
        hit = routes_ref[k : k + 1, :] == s_e
        named = jnp.where(hit, 1.0, named)
        gate = jnp.where(hit, gates_ref[k : k + 1, :].astype(F32), gate)
    t_row = lax.broadcasted_iota(jnp.int32, (z.tok, z.tok), 0)
    t_col = lax.broadcasted_iota(jnp.int32, (z.tok, z.tok), 1)
    rank = dot_nn(named.astype(BF16), onehot(t_row < t_col))
    picked = jnp.where(rank == s_rank.astype(F32), named, 0.0)
    place_ref[...] = picked.astype(BF16)
    sel[0, :, 0:LANES] = dot_nn(
        (picked * gate).astype(BF16), jnp.ones((z.tok, LANES), BF16)
    ).astype(BF16)
    for q in range(mix):
        xc[1 + q] = tok_ref[:, q * CW : (q + 1) * CW]
        xc[1 + mix + q] = dy_ref[:, q * CW : (q + 1) * CW]

    def choose(q):
        sel[q] = dot_nn(place_ref[...], xc[q]).astype(BF16)

    choose(1)

    pl.semaphore_wait(barrier, n_dp - 1 + n_x - 1 + 2)

    def remote(src, dst, send, recv, dev):
        return pltpu.make_async_remote_copy(
            src_ref=src, dst_ref=dst, send_sem=send, recv_sem=recv,
            device_id=dev, device_id_type=MESH,
        )

    def got(region, sem):
        remote(region, region, sem, sem, dev_up).wait_recv()

    def left(region, sem):
        remote(region, region, sem, sem, dev_up).wait_send()

    def f0(q, w):
        cs = pl.ds(0, w)
        if w == CW:
            pl.when(q > 1)(functools.partial(choose, q))
        mine = pl.ds(pl.multiple_of(x * xb, 16), xb)
        rx[q, mine, cs] = sel[q, mine, cs]

        def send(j, c):
            to = lax.rem(x + j, n_x)
            remote(
                sel.at[q, pl.ds(pl.multiple_of(to * xb, 16), xb), cs], rx.at[q, mine, cs],
                xs.at[q], xr.at[q], (dp, to, y),
            ).start()
            return c

        lax.fori_loop(1, n_x, send, 0)

    def f1(q, w):
        cs = pl.ds(0, w)
        got(rx.at[q, pl.ds(0, rows - xb), cs], xr.at[q])
        sd[q, :, cs] = dot_nn(mats[0], rx[q, :, cs]).astype(BF16)
        mine = pl.ds(pl.multiple_of(dp * db, 16), db)

        def send(j, c):
            to = lax.rem(dp + j, n_dp)
            remote(
                sd.at[q, pl.ds(pl.multiple_of(to * db, 16), db), cs], g.at[q, y, mine, cs],
                ds_.at[q], dr.at[q], (to, x, y),
            ).start()
            return c

        lax.fori_loop(1, n_dp, send, 0)
        g[q, y, mine, cs] = sd[q, mine, cs]

    def f2(q, w):
        cs = pl.ds(0, w)
        got(g.at[q, y, pl.ds(0, rows - db), cs], dr.at[q])
        whole = g.at[q, y, :, cs]
        remote(whole, whole, ys.at[q], yra.at[q], dev_up).start()
        remote(whole, whole, ys.at[q], yrb.at[q], dev_down).start()

    def f3(q, w):
        cs = pl.ds(0, w)
        got(g.at[q, down, :, cs], yra.at[q])
        first = g.at[q, down, pl.ds(0, half), cs]
        remote(first, first, ys.at[q], yrc.at[q], dev_up).start()
        got(g.at[q, up, :, cs], yrb.at[q])
        second = g.at[q, up, pl.ds(half, half), cs]
        remote(second, second, ys.at[q], yrd.at[q], dev_down).start()

    def f4(q, w):
        cs = pl.ds(0, w)
        got(g.at[q, far, pl.ds(0, half), cs], yrc.at[q])
        got(g.at[q, far, pl.ds(half, half), cs], yrd.at[q])
        if w != CW:
            for o in range(4):
                gt[o] = g[q, o, :, cs].astype(F32)
            return

        @pl.when(q == 1)
        def _():
            def one(o, c):
                pg[o] = dot_nt(g[q, o], wg[:, 0:CW])
                pu[o] = dot_nt(g[q, o], wu[:, 0:CW])
                return c

            lax.fori_loop(0, 4, one, 0)

        @pl.when(jnp.logical_and(q > 1, q <= mix))
        def _():
            part = pl.ds(pl.multiple_of((q - 1) * CW, CW), CW)

            def one(o, c):
                pg[o] += dot_nt(g[q, o], wg[:, part])
                pu[o] += dot_nt(g[q, o], wu[:, part])
                return c

            lax.fori_loop(0, 4, one, 0)

        @pl.when(q == mix)
        def _():
            def one(o, c):
                pre_gate = pg[o]
                pre_up = pu[o]
                sig = 1.0 / (1.0 + jnp.exp(-pre_gate))
                act = pre_gate * sig
                hidden = act * pre_up
                pg[o] = act
                pu[o] = pre_up * sig * (1.0 + pre_gate * (1.0 - sig))
                hf[o] = hidden
                f_row = lax.broadcasted_iota(jnp.int32, (z.ff, z.ff), 0)
                f_col = lax.broadcasted_iota(jnp.int32, (z.ff, z.ff), 1)
                ht[o] = dot_nt(onehot(f_row == f_col), hidden.astype(BF16)).astype(BF16)
                return c

            lax.fori_loop(0, 4, one, 0)

        @pl.when(q == mix + 1)
        def _():
            def one(o, c):
                bh[o] = dot_nt(g[q, o], wd[0])
                return c

            lax.fori_loop(0, 4, one, 0)

        @pl.when(q > mix + 1)
        def _():
            def one(o, c):
                bh[o] += dot_nt(g[q, o], wd[q - mix - 1])
                return c

            lax.fori_loop(0, 4, one, 0)

        pl.when(jnp.logical_and(q > mix, q < z.fwd - 1))(functools.partial(grad_down, q))

    def grad_down(q):
        j = q - mix - 1
        cols = pl.ds(pl.multiple_of(j * CW, CW), CW)

        def weighted(o):
            scale = jnp.concatenate([gt[o]] * 2, axis=1)
            return (scale * g[q, o].astype(F32)).astype(BF16)

        total = dot_nn(ht[0], weighted(0))
        for o in range(1, 4):
            total += dot_nn(ht[o], weighted(o))
        out_down[:, cols] = total
        down_copy(j).start()

    def at(t, do):
        pl.when(t == 0)(functools.partial(do, t, LANES))
        pl.when(jnp.logical_and(t > 0, t < z.fwd))(functools.partial(do, t, CW))

    f0(0, LANES)
    for q in range(1, AHEAD):
        f0(jnp.int32(q), CW)
    pt[...] = dot_nt(onehot(t_row == t_col), place_ref[...]).astype(BF16)
    i_row = lax.broadcasted_iota(jnp.int32, (rows, rows), 0)
    i_col = lax.broadcasted_iota(jnp.int32, (rows, rows), 1)

    def reordered(i):
        return (
            ((i & (db - 1)) >> log2(cap)) * xb + (i >> log2(db)) * cap + (i & (cap - 1))
        )

    mats[0] = onehot(i_col == reordered(i_row))
    mats[1] = onehot(i_row == reordered(i_col))


    for i in range(2 + mix):
        wcopy(i).wait()

    def tick_out(t, c):
        at(t - 4, f3)
        at(t - 2, f2)
        at(t, f1)
        pl.when(t + AHEAD < z.fwd)(functools.partial(f0, t + AHEAD, CW))
        at(t - 5, f4)
        return c

    lax.fori_loop(0, z.fwd + 5, tick_out, 0)

    def middle(o):
        back_h = bh[o]
        scaled = gt[o][:, 0:1] * back_h
        gg[o] = (scaled * pu[o]).astype(BF16)
        gu[o] = (scaled * pg[o]).astype(BF16)
        gp[o] = jnp.broadcast_to(
            jnp.sum(hf[o] * back_h, axis=1, keepdims=True), (rows, LANES)
        )

    def partial_rows(o, r, w):
        if w != CW:
            return gp[o]
        part = pl.ds(pl.multiple_of(r * CW, CW), CW)
        return dot_nn(gg[o], wg[:, part]) + dot_nn(gu[o], wu[:, part])

    lo, hi = pl.ds(0, half), pl.ds(half, half)

    def r0(r, w):
        cs = pl.ds(0, w)
        os_[r, :, cs] = partial_rows(far, r, w).astype(BF16)
        remote(os_.at[r, lo, cs], ora.at[r, :, cs], os_s.at[r], ora_r.at[r], dev_down).start()
        remote(os_.at[r, hi, cs], orb.at[r, :, cs], os_s.at[r], orb_r.at[r], dev_up).start()

    def r1(r, w):
        cs = pl.ds(0, w)
        mine = partial_rows(down, r, w)
        got(ora.at[r, :, cs], ora_r.at[r])
        am[r, lo, cs] = (mine[0:half] + ora[r, :, cs].astype(F32)).astype(BF16)
        am[r, hi, cs] = mine[half:].astype(BF16)
        remote(am.at[r, :, cs], arp.at[r, :, cs], a_s.at[r], arp_r.at[r], dev_down).start()
        mine = partial_rows(up, r, w)
        got(orb.at[r, :, cs], orb_r.at[r])
        ap[r, lo, cs] = mine[0:half].astype(BF16)
        ap[r, hi, cs] = (mine[half:] + orb[r, :, cs].astype(F32)).astype(BF16)
        remote(ap.at[r, :, cs], arm.at[r, :, cs], a_s.at[r], arm_r.at[r], dev_up).start()

    def r2(r, w):
        cs = pl.ds(0, w)
        mine = partial_rows(y, r, w)
        got(arp.at[r, :, cs], arp_r.at[r])
        got(arm.at[r, :, cs], arm_r.at[r])
        rd[r, :, cs] = (
            mine + arp[r, :, cs].astype(F32) + arm[r, :, cs].astype(F32)
        ).astype(BF16)
        own = pl.ds(pl.multiple_of(dp * db, 16), db)

        def send(j, c):
            to = lax.rem(dp + j, n_dp)
            remote(
                rd.at[r, pl.ds(pl.multiple_of(to * db, 16), db), cs], rb.at[r, own, cs],
                rd_s.at[r], rb_r.at[r], (to, x, y),
            ).start()
            return c

        lax.fori_loop(1, n_dp, send, 0)
        rb[r, own, cs] = rd[r, own, cs]

    def r3(r, w):
        cs = pl.ds(0, w)
        got(rb.at[r, pl.ds(0, rows - db), cs], rb_r.at[r])
        sx[r, :, cs] = dot_nn(mats[1], rb[r, :, cs]).astype(BF16)
        own = pl.ds(pl.multiple_of(x * xb, 16), xb)

        def send(j, c):
            to = lax.rem(x + j, n_x)
            remote(
                sx.at[r, pl.ds(pl.multiple_of(to * xb, 16), xb), cs], hb.at[r, own, cs],
                sx_s.at[r], hb_r.at[r], (dp, to, y),
            ).start()
            return c

        lax.fori_loop(1, n_x, send, 0)
        hb[r, own, cs] = sx[r, own, cs]

    def r4(r, w):
        got(hb.at[r, pl.ds(0, rows - xb), pl.ds(0, w)], hb_r.at[r])
        if w == CW:
            cols = pl.ds(pl.multiple_of(r * CW, LANES), CW)
            out_tok[:, cols] = dot_nn(pt[...], hb[r]).astype(BF16)
            return
        row = lax.broadcasted_iota(jnp.int32, (rows, LANES), 0)
        lane = lax.broadcasted_iota(jnp.int32, (rows, LANES), 1)
        e = ((row & (xb - 1)) >> log2(cap)) * n_x + (row >> log2(xb))
        vals = jnp.where(e == lane, hb[r, :, 0:LANES].astype(F32), 0.0)
        by_expert = dot_nn(pt[...], vals.astype(BF16))
        e_row = lax.broadcasted_iota(jnp.int32, (LANES, LANES), 0)
        e_col = lax.broadcasted_iota(jnp.int32, (LANES, LANES), 1)
        by_expert = dot_nt(onehot(e_row == e_col), by_expert.astype(BF16))
        e_tok = lax.broadcasted_iota(jnp.int32, (LANES, z.tok), 0)
        for k in range(z.top):
            hit = routes_ref[k : k + 1, :] == e_tok
            out_gate[k : k + 1, :] = jnp.sum(
                jnp.where(hit, by_expert, 0.0), axis=0, keepdims=True
            ).astype(BF16)

    def back(t, do):
        pl.when(jnp.logical_and(t >= 0, t < mix))(functools.partial(do, t, CW))
        pl.when(t == mix)(functools.partial(do, t, LANES))

    def tick_back(t, c):
        back(t - 2, r1)
        back(t, r0)
        back(t - 4, r2)
        back(t - 6, r3)
        back(t - 8, r4)
        return c

    middle(far)
    r0(0, CW)
    for o in (down, up, y):
        middle(o)
    grad_down(z.fwd - 1)
    lax.fori_loop(1, z.ret + 8, tick_back, 0)

    def drain_out(q, w):
        cs = pl.ds(0, w)
        left(sel.at[q, pl.ds(0, rows - xb), cs], xs.at[q])
        left(sd.at[q, pl.ds(0, rows - db), cs], ds_.at[q])
        left(g.at[q, pl.ds(0, 3), :, cs], ys.at[q])

    def drain_back(r, w):
        cs = pl.ds(0, w)
        left(os_.at[r, :, cs], os_s.at[r])
        left(g.at[r, pl.ds(0, 2), :, cs], a_s.at[r])
        left(rd.at[r, pl.ds(0, rows - db), cs], rd_s.at[r])
        left(sx.at[r, pl.ds(0, rows - xb), cs], sx_s.at[r])

    drain_out(0, LANES)
    for q in range(1, z.fwd):
        drain_out(q, CW)
    for j in range(mix):
        down_copy(j).wait()
    for r in range(mix):
        drain_back(r, CW)
    drain_back(mix, LANES)


def hand_over(tok_in, gate_in, down_in, tok_out, gate_out, down_out, tok, gate, down, sem):
    parts = [(tok_in, tok, tok_out), (gate_in, gate, gate_out)]
    step = down.shape[0] // 4
    for i in range(4):
        part = pl.ds(i * step, step)
        parts.append((down_in.at[part], down.at[part], down_out.at[part]))
    reads = [
        pltpu.make_async_copy(a, b, sem.at[0, i]) for i, (a, b, _) in enumerate(parts)
    ]
    writes = [
        pltpu.make_async_copy(b, c, sem.at[1, i]) for i, (_, b, c) in enumerate(parts)
    ]
    for read in reads:
        read.start()
    for read, write in zip(reads, writes):
        read.wait()
        write.start()
    for write in writes:
        write.wait()


def body(cap, tokens, out_grad, routes, gates, w_gate, w_up, w_down):
    z = Sizes(
        n_dp=lax.axis_size("dp"), n_x=lax.axis_size("expert"), tok=tokens.shape[0],
        top=routes.shape[1], cap=cap, width=tokens.shape[1], ff=w_gate.shape[2],
    )
    assert lax.axis_size("tensor") == 4 and z.width % CW == 0
    rows, half, fwd, ret, mix = z.rows, z.rows // 2, z.fwd, z.ret, z.mix
    vm = pltpu.VMEM
    sem = pltpu.SemaphoreType.DMA
    scratch = [
        vm((z.ff, z.width), F32),
        vm((rows, z.tok), BF16),
        vm((fwd, z.tok, CW), BF16),
        vm((fwd, rows, CW), BF16),
        vm((fwd, rows, CW), BF16),
        vm((fwd, rows, CW), BF16),
        vm((fwd, 4, rows, CW), BF16),
        vm((z.ff, z.width), BF16),
        vm((z.ff, z.width), BF16),
        vm((mix, z.ff, CW), BF16),
        vm((4, rows, z.ff), F32),
        vm((4, rows, z.ff), F32),
        vm((4, rows, z.ff), F32),
        vm((4, z.ff, rows), BF16),
        vm((4, rows, z.ff), F32),
        vm((4, rows, LANES), F32),
        vm((4, rows, z.ff), BF16),
        vm((4, rows, z.ff), BF16),
        vm((4, rows, LANES), F32),
        vm((2, rows, rows), BF16),
        vm((z.tok, rows), BF16),
        vm((ret, rows, CW), BF16),
        vm((ret, half, CW), BF16),
        vm((ret, half, CW), BF16),
        vm((ret, rows, CW), BF16),
        vm((ret, rows, CW), BF16),
        vm((ret, rows, CW), BF16),
        vm((ret, rows, CW), BF16),
        vm((ret, rows, CW), BF16),
        vm((ret, rows, CW), BF16),
        vm((ret, rows, CW), BF16),
        vm((ret, rows, CW), BF16),
        sem((2 + mix,)),
        sem((mix,)),
    ] + [sem((fwd,))] * 9 + [sem((ret,))] * 10
    vmem = pl.BlockSpec(memory_space=pltpu.VMEM)
    hbm = pl.BlockSpec(memory_space=pl.ANY)
    grad_tokens, grad_gate, grad_down = pl.pallas_call(
        functools.partial(kernel, z),
        out_shape=(
            jax.ShapeDtypeStruct((z.tok, z.width), BF16),
            jax.ShapeDtypeStruct((z.top, z.tok), BF16),
            jax.ShapeDtypeStruct((z.ff, z.width), F32),
        ),
        in_specs=[vmem] * 4 + [hbm] * 3,
        out_specs=(vmem, vmem, hbm),
        scratch_shapes=scratch,
        compiler_params=pltpu.CompilerParams(
            collective_id=0, has_side_effects=True, vmem_limit_bytes=60 * 1024 * 1024
        ),
    )(routes.T, gates.T, tokens, out_grad, w_gate[0].T, w_up[0].T, w_down[0])
    results = (grad_tokens, grad_gate, grad_down)
    grad_tokens, grad_gate, grad_down = pl.pallas_call(
        hand_over,
        out_shape=tuple(jax.ShapeDtypeStruct(r.shape, r.dtype) for r in results),
        in_specs=[hbm] * 3,
        out_specs=(hbm,) * 3,
        scratch_shapes=[vm(r.shape, r.dtype) for r in results] + [sem((2, 6))],
    )(*results)
    return grad_tokens, grad_gate.T, grad_down[None]


def solution(mesh, cap=4):
    tokens = P(("dp", "expert", "tensor"), None)
    return jax.shard_map(
        functools.partial(body, cap),
        mesh=mesh,
        in_specs=(
            tokens, tokens, tokens, tokens,
            P(("dp", "expert"), None, "tensor"),
            P(("dp", "expert"), None, "tensor"),
            P(("dp", "expert"), "tensor", None),
        ),
        out_specs=(tokens, tokens, P(("dp", "expert"), "tensor", None)),
        check_vma=False,
    )
```

```python
import dataclasses
import functools

import jax
import jax.numpy as jnp
from jax import lax
from jax.experimental import pallas as pl
from jax.experimental.pallas import tpu as pltpu
from jax.sharding import PartitionSpec as P

MESH = pl.DeviceIdType.MESH
F32 = jnp.float32
BF16 = jnp.bfloat16
LANES = 128
CW = 2 * LANES
LATE = 2
AHEAD = 4
LAGS = (3, 5, 6)
B_START, B_STEP, B_X = 3, 2, 3


@dataclasses.dataclass(frozen=True)
class Sizes:
    n_dp: int
    n_x: int
    tok: int
    top: int
    cap: int
    width: int
    ff: int
    late: int

    @property
    def rows(self):
        return self.n_dp * self.n_x * self.cap

    @property
    def mix(self):
        return self.width // CW

    @property
    def fwd(self):
        return 2 * self.mix + 1

    @property
    def early(self):
        return self.fwd - self.late

    @property
    def n_z(self):
        return self.n_dp // 2

    @property
    def ret(self):
        return self.mix + 1


def dot_nn(a, b):
    return lax.dot_general(a, b, (((1,), (0,)), ((), ())), preferred_element_type=F32)


def dot_nt(a, b):
    return lax.dot_general(a, b, (((1,), (1,)), ((), ())), preferred_element_type=F32)


def onehot(cond):
    return jnp.where(cond, 1.0, 0.0).astype(BF16)


def log2(n):
    assert n & (n - 1) == 0
    return n.bit_length() - 1


def kernel(
    z, routes_ref, gates_ref, tok_ref, dy_ref, wg_hbm, wu_hbm, wd_hbm,
    out_tok, out_gate, down_hbm,
    out_down, place_ref, xc, sel, rx, sd, g, wg, wu, wd, pg, pu, hf, ht, bh, gt, gg, gu, gp, mats, pt,
    os_, ora, orb, am, ap, arp, arm, rd, rb, sx, hb,
    tb, pmy, pmd, mb, pick, bsel, bx,
    by_s, by_r, bu_r, bd_r, bz_s, bs_s, bs_r, bx_s, bx_r, pm_s, pm_r, mb_s, mb_r,
    w_sem, d_sem, xs, xr, ds_, dr, ys, yra, yrb, yrc, yrd,
    os_s, ora_r, orb_r, a_s, arp_r, arm_r, rd_s, rb_r, sx_s, hb_r,
):
    dp = lax.axis_index("dp")
    x = lax.axis_index("expert")
    y = lax.axis_index("tensor")
    rows, cap, n_dp, n_x, mix = z.rows, z.cap, z.n_dp, z.n_x, z.mix
    half = rows // 2
    xb, db = n_dp * cap, n_x * cap
    up, down, far = lax.rem(y + 1, 4), lax.rem(y + 3, 4), lax.rem(y + 2, 4)
    dev_up, dev_down, dev_far = (dp, x, up), (dp, x, down), (dp, x, far)
    iz, ic = lax.div(dp, 2), lax.rem(dp, 2)
    n_z = z.n_z
    z_up, z_down = lax.rem(iz + 1, n_z), lax.rem(iz + n_z - 1, n_z)
    dev_zup, dev_zdown = (2 * z_up + ic, x, y), (2 * z_down + ic, x, y)
    dev_twin = (2 * iz + 1 - ic, x, y)

    def wcopy(i):
        if i == 0:
            return pltpu.make_async_copy(wg_hbm, wg, w_sem.at[0])
        if i == 1:
            return pltpu.make_async_copy(wu_hbm, wu, w_sem.at[1])
        j = i - 2
        return pltpu.make_async_copy(
            wd_hbm.at[:, pl.ds(j * CW, CW)], wd.at[j], w_sem.at[i]
        )

    def down_copy(j):
        cols = pl.ds(pl.multiple_of(j * CW, CW), CW)
        return pltpu.make_async_copy(out_down.at[:, cols], down_hbm.at[:, cols], d_sem.at[j])

    for i in range(2 + mix):
        wcopy(i).start()

    barrier = pltpu.get_barrier_semaphore()

    def greet_dp(j, c):
        pl.semaphore_signal(
            barrier, inc=1, device_id=(lax.rem(dp + j, n_dp), x, y), device_id_type=MESH
        )
        return c

    def greet_x(j, c):
        pl.semaphore_signal(
            barrier, inc=1, device_id=(dp, lax.rem(x + j, n_x), y), device_id_type=MESH
        )
        return c

    lax.fori_loop(1, n_dp, greet_dp, 0)
    lax.fori_loop(1, n_x, greet_x, 0)
    pl.semaphore_signal(barrier, inc=1, device_id=dev_up, device_id_type=MESH)
    pl.semaphore_signal(barrier, inc=1, device_id=dev_down, device_id_type=MESH)
    pl.semaphore_signal(barrier, inc=1, device_id=dev_far, device_id_type=MESH)

    slot = lax.broadcasted_iota(jnp.int32, (rows, z.tok), 0)
    s_x = slot >> log2(xb)
    s_dp = (slot & (xb - 1)) >> log2(cap)
    s_rank = slot & (cap - 1)
    s_e = s_dp * n_x + s_x
    named = jnp.zeros((rows, z.tok), F32)
    gate = jnp.zeros((rows, z.tok), F32)
    for k in range(z.top):
        hit = routes_ref[k : k + 1, :] == s_e
        named = jnp.where(hit, 1.0, named)
        gate = jnp.where(hit, gates_ref[k : k + 1, :].astype(F32), gate)
    t_row = lax.broadcasted_iota(jnp.int32, (z.tok, z.tok), 0)
    t_col = lax.broadcasted_iota(jnp.int32, (z.tok, z.tok), 1)
    rank = dot_nn(named.astype(BF16), onehot(t_row < t_col))
    picked = jnp.where(rank == s_rank.astype(F32), named, 0.0)
    place_ref[...] = picked.astype(BF16)
    sel[0, :, 0:LANES] = dot_nn(
        (picked * gate).astype(BF16), jnp.ones((z.tok, LANES), BF16)
    ).astype(BF16)
    for q in range(mix):
        xc[1 + q] = tok_ref[:, q * CW : (q + 1) * CW]
        xc[1 + mix + q] = dy_ref[:, q * CW : (q + 1) * CW]

    def choose(q):
        sel[q] = dot_nn(place_ref[...], xc[q]).astype(BF16)

    choose(1)

    for b in range(z.late):
        tb[b, y, iz, ic] = dy_ref[:, (mix - z.late + b) * CW : (mix - z.late + b + 1) * CW]
    l_row = lax.broadcasted_iota(jnp.int32, (z.tok, LANES), 0)
    l_col = lax.broadcasted_iota(jnp.int32, (z.tok, LANES), 1)
    pmy[y] = dot_nn(place_ref[...], onehot(l_col == l_row + y * z.tok)).astype(BF16)

    pl.semaphore_wait(barrier, n_dp - 1 + n_x - 1 + 3)

    def remote(src, dst, send, recv, dev):
        return pltpu.make_async_remote_copy(
            src_ref=src, dst_ref=dst, send_sem=send, recv_sem=recv,
            device_id=dev, device_id_type=MESH,
        )

    def got(region, sem):
        remote(region, region, sem, sem, dev_up).wait_recv()

    def left(region, sem):
        remote(region, region, sem, sem, dev_up).wait_send()

    def f0(q, w):
        cs = pl.ds(0, w)
        if w == CW:
            pl.when(q > 1)(functools.partial(choose, q))
        mine = pl.ds(pl.multiple_of(x * xb, 16), xb)
        rx[q, mine, cs] = sel[q, mine, cs]

        def send(j, c):
            to = lax.rem(x + j, n_x)
            remote(
                sel.at[q, pl.ds(pl.multiple_of(to * xb, 16), xb), cs], rx.at[q, mine, cs],
                xs.at[q], xr.at[q], (dp, to, y),
            ).start()
            return c

        lax.fori_loop(1, n_x, send, 0)

    def f1(q, w):
        cs = pl.ds(0, w)
        got(rx.at[q, pl.ds(0, rows - xb), cs], xr.at[q])
        sd[q, :, cs] = dot_nn(mats[0], rx[q, :, cs]).astype(BF16)
        mine = pl.ds(pl.multiple_of(dp * db, 16), db)

        def send(j, c):
            to = lax.rem(dp + j, n_dp)
            remote(
                sd.at[q, pl.ds(pl.multiple_of(to * db, 16), db), cs], g.at[q, y, mine, cs],
                ds_.at[q], dr.at[q], (to, x, y),
            ).start()
            return c

        lax.fori_loop(1, n_dp, send, 0)
        g[q, y, mine, cs] = sd[q, mine, cs]

    def f2(q, w):
        cs = pl.ds(0, w)
        got(g.at[q, y, pl.ds(0, rows - db), cs], dr.at[q])
        whole = g.at[q, y, :, cs]
        remote(whole, whole, ys.at[q], yra.at[q], dev_up).start()
        remote(whole, whole, ys.at[q], yrb.at[q], dev_down).start()

    def f3(q, w):
        cs = pl.ds(0, w)
        got(g.at[q, down, :, cs], yra.at[q])
        first = g.at[q, down, pl.ds(0, half), cs]
        remote(first, first, ys.at[q], yrc.at[q], dev_up).start()
        got(g.at[q, up, :, cs], yrb.at[q])
        second = g.at[q, up, pl.ds(half, half), cs]
        remote(second, second, ys.at[q], yrd.at[q], dev_down).start()

    def f4(q, w):
        cs = pl.ds(0, w)
        got(g.at[q, far, pl.ds(0, half), cs], yrc.at[q])
        got(g.at[q, far, pl.ds(half, half), cs], yrd.at[q])
        if w != CW:
            for o in range(4):
                gt[o] = g[q, o, :, cs].astype(F32)
            return
        multiply(q)

    def multiply(q):
        @pl.when(q == 1)
        def _():
            def one(o, c):
                pg[o] = dot_nt(g[q, o], wg[:, 0:CW])
                pu[o] = dot_nt(g[q, o], wu[:, 0:CW])
                return c

            lax.fori_loop(0, 4, one, 0)

        @pl.when(jnp.logical_and(q > 1, q <= mix))
        def _():
            part = pl.ds(pl.multiple_of((q - 1) * CW, CW), CW)

            def one(o, c):
                pg[o] += dot_nt(g[q, o], wg[:, part])
                pu[o] += dot_nt(g[q, o], wu[:, part])
                return c

            lax.fori_loop(0, 4, one, 0)

        @pl.when(q == mix)
        def _():
            def one(o, c):
                pre_gate = pg[o]
                pre_up = pu[o]
                sig = 1.0 / (1.0 + jnp.exp(-pre_gate))
                act = pre_gate * sig
                hidden = act * pre_up
                pg[o] = act
                pu[o] = pre_up * sig * (1.0 + pre_gate * (1.0 - sig))
                hf[o] = hidden
                f_row = lax.broadcasted_iota(jnp.int32, (z.ff, z.ff), 0)
                f_col = lax.broadcasted_iota(jnp.int32, (z.ff, z.ff), 1)
                ht[o] = dot_nt(onehot(f_row == f_col), hidden.astype(BF16)).astype(BF16)
                return c

            lax.fori_loop(0, 4, one, 0)

        @pl.when(q == mix + 1)
        def _():
            def one(o, c):
                bh[o] = dot_nt(g[q, o], wd[0])
                return c

            lax.fori_loop(0, 4, one, 0)

        @pl.when(q > mix + 1)
        def _():
            def one(o, c):
                bh[o] += dot_nt(g[q, o], wd[q - mix - 1])
                return c

            lax.fori_loop(0, 4, one, 0)

        pl.when(jnp.logical_and(q > mix, q != z.early - 1))(functools.partial(grad_down, q))

    def grad_down(q):
        j = q - mix - 1
        cols = pl.ds(pl.multiple_of(j * CW, CW), CW)

        def weighted(o):
            scale = jnp.concatenate([gt[o]] * 2, axis=1)
            return (scale * g[q, o].astype(F32)).astype(BF16)

        total = dot_nn(ht[0], weighted(0))
        for o in range(1, 4):
            total += dot_nn(ht[o], weighted(o))
        out_down[:, cols] = total
        down_copy(j).start()

    def at(t, do):
        pl.when(t == 0)(functools.partial(do, t, LANES))
        pl.when(jnp.logical_and(t > 0, t < z.early))(functools.partial(do, t, CW))

    def spread():
        for b in range(z.late):
            own = tb.at[b, y, iz, ic]
            for dev in (dev_up, dev_down, dev_far):
                remote(own, own, by_s.at[b], by_r.at[b], dev).start()
        for dev in (dev_up, dev_down, dev_far):
            remote(pmy.at[y], pmy.at[y], pm_s.at[0], pm_r.at[0], dev).start()

    def share_places():
        got(pmy.at[pl.ds(0, 3)], pm_r.at[0])
        places = pmy[0] + pmy[1] + pmy[2] + pmy[3]
        pmd[...] = dot_nn(mats[0], places).astype(BF16)
        mine = pl.ds(pl.multiple_of(dp * db, 16), db)

        def send(j, c):
            to = lax.rem(dp + j, n_dp)
            remote(
                pmd.at[pl.ds(pl.multiple_of(to * db, 16), db)], mb.at[mine],
                mb_s.at[0], mb_r.at[0], (to, x, y),
            ).start()
            return c

        lax.fori_loop(1, n_dp, send, 0)
        mb[mine] = pmd[mine]

    def make_picks():
        got(mb.at[pl.ds(0, rows - db)], mb_r.at[0])
        k_row = lax.broadcasted_iota(jnp.int32, (LANES, LANES), 0)
        k_col = lax.broadcasted_iota(jnp.int32, (LANES, LANES), 1)
        same = (k_row >> log2(z.tok)) == (k_col >> log2(z.tok))
        count = jnp.where(same, ((k_row & (z.tok - 1)) + 1).astype(F32), 0.0)
        numbers = dot_nn(mb[...], count.astype(BF16)).astype(BF16)
        numbers = dot_nn(mats[1], numbers)
        p_row = lax.broadcasted_iota(jnp.int32, (rows, n_dp * z.tok), 0)
        p_col = lax.broadcasted_iota(jnp.int32, (rows, n_dp * z.tok), 1)
        first = ((p_row & (xb - 1)) >> log2(cap)) * z.tok
        number = (p_col - first + 1).astype(F32)
        for o in range(4):
            found = numbers[:, o * z.tok : o * z.tok + 1]
            pick[o] = onehot(jnp.logical_and(number == found, found > 0.0))

    n_ring = n_z // 2

    def ring_send(b, s):
        block_up = lax.rem(iz + n_z - (s - 1), n_z)
        block_down = lax.rem(iz + (s - 1), n_z)
        some_up, some_down = (0, 4), (0, 4)
        if s == n_ring:
            some_up, some_down = (0, 2), (2, 2)
        a = tb.at[b, pl.ds(*some_up), block_up, ic]
        remote(a, a, bz_s.at[b], bu_r.at[b, s - 1], dev_zup).start()
        a = tb.at[b, pl.ds(*some_down), block_down, ic]
        remote(a, a, bz_s.at[b], bd_r.at[b, s - 1], dev_zdown).start()

    def ring_got(b, s):
        block_up = lax.rem(iz + n_z - s, n_z)
        block_down = lax.rem(iz + s, n_z)
        some_up, some_down = (0, 4), (0, 4)
        if s == n_ring:
            some_up, some_down = (0, 2), (2, 2)
        got(tb.at[b, pl.ds(*some_up), block_up, ic], bu_r.at[b, s - 1])
        got(tb.at[b, pl.ds(*some_down), block_down, ic], bd_r.at[b, s - 1])

    def b_ring(s, b):
        if s == 0:
            got(tb.at[b, pl.ds(0, 3), iz, ic], by_r.at[b])
        else:
            ring_got(b, s)
        if s < n_ring:
            ring_send(b, s + 1)
        else:
            a = tb.at[b, :, :, ic]
            remote(a, a, bs_s.at[b], bs_r.at[b], dev_twin).start()

    def b_select(b):
        got(tb.at[b, :, :, 1 - ic], bs_r.at[b])
        mine = pl.ds(pl.multiple_of(x * xb, 16), xb)

        def one(o, c):
            bsel[b, o] = dot_nn(pick[o], tb[b, o].reshape(n_dp * z.tok, CW)).astype(BF16)
            bx[b, o, mine] = bsel[b, o, mine]

            def send(j, c):
                to = lax.rem(x + j, n_x)
                remote(
                    bsel.at[b, o, pl.ds(pl.multiple_of(to * xb, 16), xb)], bx.at[b, o, mine],
                    bx_s.at[b], bx_r.at[b], (dp, to, y),
                ).start()
                return c

            return lax.fori_loop(1, n_x, send, c)

        lax.fori_loop(0, 4, one, 0)

    def b_place(b):
        got(bx.at[b, :, pl.ds(0, rows - xb)], bx_r.at[b])

        def one(o, c):
            g[z.early + b, o] = dot_nn(mats[0], bx[b, o]).astype(BF16)
            return c

        lax.fori_loop(0, 4, one, 0)

    def b_multiply(b):
        multiply(z.early + b)

    def when_b(t, start, stride, do):
        u = t - start
        on = jnp.logical_and(u >= 0, u < stride * z.late)
        if stride > 1:
            on = jnp.logical_and(on, lax.rem(u + stride * z.late, stride) == 0)
        pl.when(on)(lambda: do(lax.div(u, stride)))

    f0(0, LANES)
    f0(jnp.int32(1), CW)
    spread()
    for q in range(2, min(AHEAD, z.early)):
        f0(jnp.int32(q), CW)
    pt[...] = dot_nt(onehot(t_row == t_col), place_ref[...]).astype(BF16)
    i_row = lax.broadcasted_iota(jnp.int32, (rows, rows), 0)
    i_col = lax.broadcasted_iota(jnp.int32, (rows, rows), 1)

    def reordered(i):
        return (
            ((i & (db - 1)) >> log2(cap)) * xb + (i >> log2(db)) * cap + (i & (cap - 1))
        )

    mats[0] = onehot(i_col == reordered(i_row))
    mats[1] = onehot(i_row == reordered(i_col))


    for i in range(2 + mix):
        wcopy(i).wait()

    t_sel = B_START + B_STEP * n_ring + 1
    t_place = t_sel + B_X
    t_mul = max(t_place + (B_STEP - 1) * (z.late - 1) + 1, mix + LAGS[2] + 2)

    def tick_out(t, c):
        at(t - LAGS[1], f3)
        at(t - LAGS[0], f2)
        at(t, f1)
        pl.when(t + AHEAD < z.early)(functools.partial(f0, t + AHEAD, CW))
        at(t - LAGS[2], f4)
        for s in range(n_ring + 1):
            when_b(t, B_START + B_STEP * s, B_STEP, functools.partial(b_ring, s))
        pl.when(t == B_START)(share_places)
        pl.when(t == t_sel - 1)(make_picks)
        when_b(t, t_sel, B_STEP, b_select)
        when_b(t, t_place, B_STEP, b_place)
        when_b(t, t_mul, 1, b_multiply)
        return c

    lax.fori_loop(0, max(z.early + LAGS[2], t_mul + z.late), tick_out, 0)

    def middle(o):
        back_h = bh[o]
        scaled = gt[o][:, 0:1] * back_h
        gg[o] = (scaled * pu[o]).astype(BF16)
        gu[o] = (scaled * pg[o]).astype(BF16)
        gp[o] = jnp.broadcast_to(
            jnp.sum(hf[o] * back_h, axis=1, keepdims=True), (rows, LANES)
        )

    def partial_rows(o, r, w):
        if w != CW:
            return gp[o]
        part = pl.ds(pl.multiple_of(r * CW, CW), CW)
        return dot_nn(gg[o], wg[:, part]) + dot_nn(gu[o], wu[:, part])

    lo, hi = pl.ds(0, half), pl.ds(half, half)

    def r0(r, w):
        cs = pl.ds(0, w)
        os_[r, :, cs] = partial_rows(far, r, w).astype(BF16)
        remote(os_.at[r, lo, cs], ora.at[r, :, cs], os_s.at[r], ora_r.at[r], dev_down).start()
        remote(os_.at[r, hi, cs], orb.at[r, :, cs], os_s.at[r], orb_r.at[r], dev_up).start()

    def r1(r, w):
        cs = pl.ds(0, w)
        mine = partial_rows(down, r, w)
        got(ora.at[r, :, cs], ora_r.at[r])
        am[r, lo, cs] = (mine[0:half] + ora[r, :, cs].astype(F32)).astype(BF16)
        am[r, hi, cs] = mine[half:].astype(BF16)
        remote(am.at[r, :, cs], arp.at[r, :, cs], a_s.at[r], arp_r.at[r], dev_down).start()
        mine = partial_rows(up, r, w)
        got(orb.at[r, :, cs], orb_r.at[r])
        ap[r, lo, cs] = mine[0:half].astype(BF16)
        ap[r, hi, cs] = (mine[half:] + orb[r, :, cs].astype(F32)).astype(BF16)
        remote(ap.at[r, :, cs], arm.at[r, :, cs], a_s.at[r], arm_r.at[r], dev_up).start()

    def r2(r, w):
        cs = pl.ds(0, w)
        mine = partial_rows(y, r, w)
        got(arp.at[r, :, cs], arp_r.at[r])
        got(arm.at[r, :, cs], arm_r.at[r])
        rd[r, :, cs] = (
            mine + arp[r, :, cs].astype(F32) + arm[r, :, cs].astype(F32)
        ).astype(BF16)
        own = pl.ds(pl.multiple_of(dp * db, 16), db)

        def send(j, c):
            to = lax.rem(dp + j, n_dp)
            remote(
                rd.at[r, pl.ds(pl.multiple_of(to * db, 16), db), cs], rb.at[r, own, cs],
                rd_s.at[r], rb_r.at[r], (to, x, y),
            ).start()
            return c

        lax.fori_loop(1, n_dp, send, 0)
        rb[r, own, cs] = rd[r, own, cs]

    def r3(r, w):
        cs = pl.ds(0, w)
        got(rb.at[r, pl.ds(0, rows - db), cs], rb_r.at[r])
        sx[r, :, cs] = dot_nn(mats[1], rb[r, :, cs]).astype(BF16)
        own = pl.ds(pl.multiple_of(x * xb, 16), xb)

        def send(j, c):
            to = lax.rem(x + j, n_x)
            remote(
                sx.at[r, pl.ds(pl.multiple_of(to * xb, 16), xb), cs], hb.at[r, own, cs],
                sx_s.at[r], hb_r.at[r], (dp, to, y),
            ).start()
            return c

        lax.fori_loop(1, n_x, send, 0)
        hb[r, own, cs] = sx[r, own, cs]

    def r4(r, w):
        got(hb.at[r, pl.ds(0, rows - xb), pl.ds(0, w)], hb_r.at[r])
        if w == CW:
            cols = pl.ds(pl.multiple_of(r * CW, LANES), CW)
            out_tok[:, cols] = dot_nn(pt[...], hb[r]).astype(BF16)
            return
        row = lax.broadcasted_iota(jnp.int32, (rows, LANES), 0)
        lane = lax.broadcasted_iota(jnp.int32, (rows, LANES), 1)
        e = ((row & (xb - 1)) >> log2(cap)) * n_x + (row >> log2(xb))
        vals = jnp.where(e == lane, hb[r, :, 0:LANES].astype(F32), 0.0)
        by_expert = dot_nn(pt[...], vals.astype(BF16))
        e_row = lax.broadcasted_iota(jnp.int32, (LANES, LANES), 0)
        e_col = lax.broadcasted_iota(jnp.int32, (LANES, LANES), 1)
        by_expert = dot_nt(onehot(e_row == e_col), by_expert.astype(BF16))
        e_tok = lax.broadcasted_iota(jnp.int32, (LANES, z.tok), 0)
        for k in range(z.top):
            hit = routes_ref[k : k + 1, :] == e_tok
            out_gate[k : k + 1, :] = jnp.sum(
                jnp.where(hit, by_expert, 0.0), axis=0, keepdims=True
            ).astype(BF16)

    def back(t, do):
        pl.when(jnp.logical_and(t >= 0, t < mix))(functools.partial(do, t, CW))
        pl.when(t == mix)(functools.partial(do, t, LANES))

    def tick_back(t, c):
        back(t - 2, r1)
        back(t, r0)
        back(t - 4, r2)
        back(t - 6, r3)
        back(t - 8, r4)
        return c

    middle(far)
    r0(0, CW)
    for o in (down, up, y):
        middle(o)
    grad_down(z.early - 1)
    lax.fori_loop(1, z.ret + 8, tick_back, 0)

    def drain_out(q, w):
        cs = pl.ds(0, w)
        left(sel.at[q, pl.ds(0, rows - xb), cs], xs.at[q])
        left(sd.at[q, pl.ds(0, rows - db), cs], ds_.at[q])
        left(g.at[q, pl.ds(0, 3), :, cs], ys.at[q])

    def drain_back(r, w):
        cs = pl.ds(0, w)
        left(os_.at[r, :, cs], os_s.at[r])
        left(g.at[r, pl.ds(0, 2), :, cs], a_s.at[r])
        left(rd.at[r, pl.ds(0, rows - db), cs], rd_s.at[r])
        left(sx.at[r, pl.ds(0, rows - xb), cs], sx_s.at[r])

    drain_out(0, LANES)
    for q in range(1, z.early):
        drain_out(q, CW)
    for b in range(z.late):
        left(tb.at[b, pl.ds(0, 3), 0, 0], by_s.at[b])
        left(tb.at[b, :, pl.ds(0, n_z - 1), 0], bz_s.at[b])
        left(tb.at[b, :, :, 0], bs_s.at[b])
        left(bx.at[b, :, pl.ds(0, rows - xb)], bx_s.at[b])
    left(pmy.at[pl.ds(0, 3)], pm_s.at[0])
    left(mb.at[pl.ds(0, rows - db)], mb_s.at[0])
    for j in range(mix):
        down_copy(j).wait()
    for r in range(mix):
        drain_back(r, CW)
    drain_back(mix, LANES)


def hand_over(tok_in, gate_in, down_in, tok_out, gate_out, down_out, tok, gate, down, sem):
    parts = [(tok_in, tok, tok_out), (gate_in, gate, gate_out)]
    step = down.shape[0] // 4
    for i in range(4):
        part = pl.ds(i * step, step)
        parts.append((down_in.at[part], down.at[part], down_out.at[part]))
    reads = [
        pltpu.make_async_copy(a, b, sem.at[0, i]) for i, (a, b, _) in enumerate(parts)
    ]
    writes = [
        pltpu.make_async_copy(b, c, sem.at[1, i]) for i, (_, b, c) in enumerate(parts)
    ]
    for read in reads:
        read.start()
    for read, write in zip(reads, writes):
        read.wait()
        write.start()
    for write in writes:
        write.wait()


def body(cap, tokens, out_grad, routes, gates, w_gate, w_up, w_down):
    z = Sizes(
        late=min(LATE, tokens.shape[1] // CW - 1),
        n_dp=lax.axis_size("dp"), n_x=lax.axis_size("expert"), tok=tokens.shape[0],
        top=routes.shape[1], cap=cap, width=tokens.shape[1], ff=w_gate.shape[2],
    )
    assert lax.axis_size("tensor") == 4 and z.width % CW == 0
    rows, half, fwd, ret, mix = z.rows, z.rows // 2, z.fwd, z.ret, z.mix
    vm = pltpu.VMEM
    sem = pltpu.SemaphoreType.DMA
    scratch = [
        vm((z.ff, z.width), F32),
        vm((rows, z.tok), BF16),
        vm((fwd, z.tok, CW), BF16),
        vm((fwd, rows, CW), BF16),
        vm((fwd, rows, CW), BF16),
        vm((fwd, rows, CW), BF16),
        vm((fwd, 4, rows, CW), BF16),
        vm((z.ff, z.width), BF16),
        vm((z.ff, z.width), BF16),
        vm((mix, z.ff, CW), BF16),
        vm((4, rows, z.ff), F32),
        vm((4, rows, z.ff), F32),
        vm((4, rows, z.ff), F32),
        vm((4, z.ff, rows), BF16),
        vm((4, rows, z.ff), F32),
        vm((4, rows, LANES), F32),
        vm((4, rows, z.ff), BF16),
        vm((4, rows, z.ff), BF16),
        vm((4, rows, LANES), F32),
        vm((2, rows, rows), BF16),
        vm((z.tok, rows), BF16),
        vm((ret, rows, CW), BF16),
        vm((ret, half, CW), BF16),
        vm((ret, half, CW), BF16),
        vm((ret, rows, CW), BF16),
        vm((ret, rows, CW), BF16),
        vm((ret, rows, CW), BF16),
        vm((ret, rows, CW), BF16),
        vm((ret, rows, CW), BF16),
        vm((ret, rows, CW), BF16),
        vm((ret, rows, CW), BF16),
        vm((ret, rows, CW), BF16),
        vm((z.late, 4, z.n_z, 2, z.tok, CW), BF16),
        vm((4, rows, LANES), BF16),
        vm((rows, LANES), BF16),
        vm((rows, LANES), BF16),
        vm((4, rows, z.n_dp * z.tok), BF16),
        vm((z.late, 4, rows, CW), BF16),
        vm((z.late, 4, rows, CW), BF16),
        sem((z.late,)), sem((z.late,)),
        sem((z.late, z.n_z // 2)), sem((z.late, z.n_z // 2)), sem((z.late,)),
        sem((z.late,)), sem((z.late,)), sem((z.late,)), sem((z.late,)),
        sem((1,)), sem((1,)), sem((1,)), sem((1,)),
        sem((2 + mix,)),
        sem((mix,)),
    ] + [sem((fwd,))] * 9 + [sem((ret,))] * 10
    vmem = pl.BlockSpec(memory_space=pltpu.VMEM)
    hbm = pl.BlockSpec(memory_space=pl.ANY)
    grad_tokens, grad_gate, grad_down = pl.pallas_call(
        functools.partial(kernel, z),
        out_shape=(
            jax.ShapeDtypeStruct((z.tok, z.width), BF16),
            jax.ShapeDtypeStruct((z.top, z.tok), BF16),
            jax.ShapeDtypeStruct((z.ff, z.width), F32),
        ),
        in_specs=[vmem] * 4 + [hbm] * 3,
        out_specs=(vmem, vmem, hbm),
        scratch_shapes=scratch,
        compiler_params=pltpu.CompilerParams(
            collective_id=0, has_side_effects=True, vmem_limit_bytes=60 * 1024 * 1024
        ),
    )(routes.T, gates.T, tokens, out_grad, w_gate[0].T, w_up[0].T, w_down[0])
    results = (grad_tokens, grad_gate, grad_down)
    grad_tokens, grad_gate, grad_down = pl.pallas_call(
        hand_over,
        out_shape=tuple(jax.ShapeDtypeStruct(r.shape, r.dtype) for r in results),
        in_specs=[hbm] * 3,
        out_specs=(hbm,) * 3,
        scratch_shapes=[vm(r.shape, r.dtype) for r in results] + [sem((2, 6))],
    )(*results)
    return grad_tokens, grad_gate.T, grad_down[None]


def solution(mesh, cap=4):
    tokens = P(("dp", "expert", "tensor"), None)
    return jax.shard_map(
        functools.partial(body, cap),
        mesh=mesh,
        in_specs=(
            tokens, tokens, tokens, tokens,
            P(("dp", "expert"), None, "tensor"),
            P(("dp", "expert"), None, "tensor"),
            P(("dp", "expert"), "tensor", None),
        ),
        out_specs=(tokens, tokens, P(("dp", "expert"), "tensor", None)),
        check_vma=False,
    )
```

```python
import dataclasses
import functools

import jax
import jax.numpy as jnp
from jax import lax
from jax.experimental import pallas as pl
from jax.experimental.pallas import tpu as pltpu
from jax.sharding import PartitionSpec as P

MESH = pl.DeviceIdType.MESH
F32 = jnp.float32
BF16 = jnp.bfloat16
LANES = 128
CW = 2 * LANES
LATE = 2
AHEAD = 4
LAGS = (3, 5, 6)
B_START, B_STEP, B_X, B_GAP = 3, 2, 3, 1


@dataclasses.dataclass(frozen=True)
class Sizes:
    n_dp: int
    n_x: int
    tok: int
    top: int
    cap: int
    width: int
    ff: int
    late: int

    @property
    def rows(self):
        return self.n_dp * self.n_x * self.cap

    @property
    def mix(self):
        return self.width // CW

    @property
    def fwd(self):
        return 2 * self.mix + 1

    @property
    def early(self):
        return self.fwd - self.late

    @property
    def n_z(self):
        return self.n_dp // 2

    @property
    def ret(self):
        return self.mix + 1


def dot_nn(a, b):
    return lax.dot_general(a, b, (((1,), (0,)), ((), ())), preferred_element_type=F32)


def dot_nt(a, b):
    return lax.dot_general(a, b, (((1,), (1,)), ((), ())), preferred_element_type=F32)


def onehot(cond):
    return jnp.where(cond, 1.0, 0.0).astype(BF16)


def log2(n):
    assert n & (n - 1) == 0
    return n.bit_length() - 1


def kernel(
    z, routes_hbm, gates_ref, tok_hbm, dy_hbm, wg_hbm, wu_hbm, wd_hbm,
    out_tok, out_gate, down_hbm,
    routes_ref, tok_ref, dy_ref, in_sem, out_down, place_ref, xc, sel, rx, sd, g, wg, wu, wd, pg, pu, hf, ht, bh, gt, gg, gu, gp, mats, pt,
    os_, ora, orb, am, ap, arp, arm, rd, rb, sx, hb,
    tb, pmy, pmd, mb, pick, bsel, bx,
    by_s, by_r, bu_r, bd_r, bz_s, bs_s, bs_r, bx_s, bx_r, pm_s, pm_r, mb_s, mb_r,
    w_sem, d_sem, xs, xr, ds_, dr, ys, yra, yrb, yrc, yrd,
    os_s, ora_r, orb_r, a_s, arp_r, arm_r, rd_s, rb_r, sx_s, hb_r,
):
    dp = lax.axis_index("dp")
    x = lax.axis_index("expert")
    y = lax.axis_index("tensor")
    rows, cap, n_dp, n_x, mix = z.rows, z.cap, z.n_dp, z.n_x, z.mix
    half = rows // 2
    xb, db = n_dp * cap, n_x * cap
    up, down, far = lax.rem(y + 1, 4), lax.rem(y + 3, 4), lax.rem(y + 2, 4)
    dev_up, dev_down, dev_far = (dp, x, up), (dp, x, down), (dp, x, far)
    iz, ic = lax.div(dp, 2), lax.rem(dp, 2)
    n_z = z.n_z
    z_up, z_down = lax.rem(iz + 1, n_z), lax.rem(iz + n_z - 1, n_z)
    dev_zup, dev_zdown = (2 * z_up + ic, x, y), (2 * z_down + ic, x, y)
    dev_twin = (2 * iz + 1 - ic, x, y)

    def wcopy(i):
        if i == 0:
            return pltpu.make_async_copy(wg_hbm, wg, w_sem.at[0])
        if i == 1:
            return pltpu.make_async_copy(wu_hbm, wu, w_sem.at[1])
        j = i - 2
        return pltpu.make_async_copy(
            wd_hbm.at[:, pl.ds(j * CW, CW)], wd.at[j], w_sem.at[i]
        )

    def down_copy(j):
        cols = pl.ds(pl.multiple_of(j * CW, CW), CW)
        return pltpu.make_async_copy(out_down.at[:, cols], down_hbm.at[:, cols], d_sem.at[j])

    reads = [
        pltpu.make_async_copy(a, b, in_sem.at[i])
        for i, (a, b) in enumerate(
            [(routes_hbm, routes_ref), (tok_hbm, tok_ref), (dy_hbm, dy_ref)]
        )
    ]
    for read in reads:
        read.start()

    barrier = pltpu.get_barrier_semaphore()

    def greet_dp(j, c):
        pl.semaphore_signal(
            barrier, inc=1, device_id=(lax.rem(dp + j, n_dp), x, y), device_id_type=MESH
        )
        return c

    def greet_x(j, c):
        pl.semaphore_signal(
            barrier, inc=1, device_id=(dp, lax.rem(x + j, n_x), y), device_id_type=MESH
        )
        return c

    lax.fori_loop(1, n_dp, greet_dp, 0)
    lax.fori_loop(1, n_x, greet_x, 0)
    pl.semaphore_signal(barrier, inc=1, device_id=dev_up, device_id_type=MESH)
    pl.semaphore_signal(barrier, inc=1, device_id=dev_down, device_id_type=MESH)
    pl.semaphore_signal(barrier, inc=1, device_id=dev_far, device_id_type=MESH)

    for i in range(2 + mix):
        wcopy(i).start()
    for read in reads:
        read.wait()

    slot = lax.broadcasted_iota(jnp.int32, (rows, z.tok), 0)
    s_x = slot >> log2(xb)
    s_dp = (slot & (xb - 1)) >> log2(cap)
    s_rank = slot & (cap - 1)
    s_e = s_dp * n_x + s_x
    gates = gates_ref[...].astype(F32)
    named = jnp.zeros((rows, z.tok), F32)
    gate = jnp.zeros((rows, z.tok), F32)
    for k in range(z.top):
        hit = routes_ref[k : k + 1, :] == s_e
        named = jnp.where(hit, 1.0, named)
        gate = jnp.where(hit, gates[k : k + 1, :], gate)
    t_row = lax.broadcasted_iota(jnp.int32, (z.tok, z.tok), 0)
    t_col = lax.broadcasted_iota(jnp.int32, (z.tok, z.tok), 1)
    rank = dot_nn(named.astype(BF16), onehot(t_row < t_col))
    picked = jnp.where(rank == s_rank.astype(F32), named, 0.0)
    place_ref[...] = picked.astype(BF16)
    sel[0, :, 0:LANES] = dot_nn(
        (picked * gate).astype(BF16), jnp.ones((z.tok, LANES), BF16)
    ).astype(BF16)
    for q in range(mix):
        xc[1 + q] = tok_ref[:, q * CW : (q + 1) * CW]
        xc[1 + mix + q] = dy_ref[:, q * CW : (q + 1) * CW]

    def choose(q):
        sel[q] = dot_nn(place_ref[...], xc[q]).astype(BF16)

    choose(1)

    for b in range(z.late):
        tb[b, y, iz, ic] = dy_ref[:, (mix - z.late + b) * CW : (mix - z.late + b + 1) * CW]
    l_row = lax.broadcasted_iota(jnp.int32, (z.tok, LANES), 0)
    l_col = lax.broadcasted_iota(jnp.int32, (z.tok, LANES), 1)
    pmy[y] = dot_nn(place_ref[...], onehot(l_col == l_row + y * z.tok)).astype(BF16)

    pl.semaphore_wait(barrier, n_dp - 1 + n_x - 1 + 3)

    def remote(src, dst, send, recv, dev):
        return pltpu.make_async_remote_copy(
            src_ref=src, dst_ref=dst, send_sem=send, recv_sem=recv,
            device_id=dev, device_id_type=MESH,
        )

    def got(region, sem):
        remote(region, region, sem, sem, dev_up).wait_recv()

    def left(region, sem):
        remote(region, region, sem, sem, dev_up).wait_send()

    def f0(q, w):
        cs = pl.ds(0, w)
        if w == CW:
            pl.when(q > 1)(functools.partial(choose, q))
        mine = pl.ds(pl.multiple_of(x * xb, 16), xb)
        rx[q, mine, cs] = sel[q, mine, cs]

        def send(j, c):
            to = lax.rem(x + j, n_x)
            remote(
                sel.at[q, pl.ds(pl.multiple_of(to * xb, 16), xb), cs], rx.at[q, mine, cs],
                xs.at[q], xr.at[q], (dp, to, y),
            ).start()
            return c

        lax.fori_loop(1, n_x, send, 0)

    def f1(q, w):
        cs = pl.ds(0, w)
        got(rx.at[q, pl.ds(0, rows - xb), cs], xr.at[q])
        sd[q, :, cs] = dot_nn(mats[0], rx[q, :, cs]).astype(BF16)
        mine = pl.ds(pl.multiple_of(dp * db, 16), db)

        def send(j, c):
            to = lax.rem(dp + j, n_dp)
            remote(
                sd.at[q, pl.ds(pl.multiple_of(to * db, 16), db), cs], g.at[q, y, mine, cs],
                ds_.at[q], dr.at[q], (to, x, y),
            ).start()
            return c

        lax.fori_loop(1, n_dp, send, 0)
        g[q, y, mine, cs] = sd[q, mine, cs]

    def f2(q, w):
        cs = pl.ds(0, w)
        got(g.at[q, y, pl.ds(0, rows - db), cs], dr.at[q])
        whole = g.at[q, y, :, cs]
        remote(whole, whole, ys.at[q], yra.at[q], dev_up).start()
        remote(whole, whole, ys.at[q], yrb.at[q], dev_down).start()

    def f3(q, w):
        cs = pl.ds(0, w)
        got(g.at[q, down, :, cs], yra.at[q])
        first = g.at[q, down, pl.ds(0, half), cs]
        remote(first, first, ys.at[q], yrc.at[q], dev_up).start()
        got(g.at[q, up, :, cs], yrb.at[q])
        second = g.at[q, up, pl.ds(half, half), cs]
        remote(second, second, ys.at[q], yrd.at[q], dev_down).start()

    def f4(q, w):
        cs = pl.ds(0, w)
        got(g.at[q, far, pl.ds(0, half), cs], yrc.at[q])
        got(g.at[q, far, pl.ds(half, half), cs], yrd.at[q])
        if w != CW:
            for o in range(4):
                gt[o] = g[q, o, :, cs].astype(F32)
            return
        multiply(q)

    def multiply(q):
        @pl.when(q == 1)
        def _():
            def one(o, c):
                pg[o] = dot_nt(g[q, o], wg[:, 0:CW])
                pu[o] = dot_nt(g[q, o], wu[:, 0:CW])
                return c

            lax.fori_loop(0, 4, one, 0)

        @pl.when(jnp.logical_and(q > 1, q <= mix))
        def _():
            part = pl.ds(pl.multiple_of((q - 1) * CW, CW), CW)

            def one(o, c):
                pg[o] += dot_nt(g[q, o], wg[:, part])
                pu[o] += dot_nt(g[q, o], wu[:, part])
                return c

            lax.fori_loop(0, 4, one, 0)

        @pl.when(q == mix)
        def _():
            def one(o, c):
                pre_gate = pg[o]
                pre_up = pu[o]
                sig = 1.0 / (1.0 + jnp.exp(-pre_gate))
                act = pre_gate * sig
                hidden = act * pre_up
                pg[o] = act
                pu[o] = pre_up * sig * (1.0 + pre_gate * (1.0 - sig))
                hf[o] = hidden
                f_row = lax.broadcasted_iota(jnp.int32, (z.ff, z.ff), 0)
                f_col = lax.broadcasted_iota(jnp.int32, (z.ff, z.ff), 1)
                ht[o] = dot_nt(onehot(f_row == f_col), hidden.astype(BF16)).astype(BF16)
                return c

            lax.fori_loop(0, 4, one, 0)

        @pl.when(q == mix + 1)
        def _():
            def one(o, c):
                bh[o] = dot_nt(g[q, o], wd[0])
                return c

            lax.fori_loop(0, 4, one, 0)

        @pl.when(q > mix + 1)
        def _():
            def one(o, c):
                bh[o] += dot_nt(g[q, o], wd[q - mix - 1])
                return c

            lax.fori_loop(0, 4, one, 0)

        pl.when(jnp.logical_and(q > mix, q != z.early - 1))(functools.partial(grad_down, q))

    def grad_down(q):
        j = q - mix - 1
        cols = pl.ds(pl.multiple_of(j * CW, CW), CW)

        def weighted(o):
            scale = jnp.concatenate([gt[o]] * 2, axis=1)
            return (scale * g[q, o].astype(F32)).astype(BF16)

        total = dot_nn(ht[0], weighted(0))
        for o in range(1, 4):
            total += dot_nn(ht[o], weighted(o))
        out_down[:, cols] = total
        down_copy(j).start()

    def at(t, do):
        pl.when(t == 0)(functools.partial(do, t, LANES))
        pl.when(jnp.logical_and(t > 0, t < z.early))(functools.partial(do, t, CW))

    def spread():
        for b in range(z.late):
            own = tb.at[b, y, iz, ic]
            for dev in (dev_up, dev_down, dev_far):
                remote(own, own, by_s.at[b], by_r.at[b], dev).start()
        for dev in (dev_up, dev_down, dev_far):
            remote(pmy.at[y], pmy.at[y], pm_s.at[0], pm_r.at[0], dev).start()

    def share_places():
        got(pmy.at[pl.ds(0, 3)], pm_r.at[0])
        places = pmy[0] + pmy[1] + pmy[2] + pmy[3]
        pmd[...] = dot_nn(mats[0], places).astype(BF16)
        mine = pl.ds(pl.multiple_of(dp * db, 16), db)

        def send(j, c):
            to = lax.rem(dp + j, n_dp)
            remote(
                pmd.at[pl.ds(pl.multiple_of(to * db, 16), db)], mb.at[mine],
                mb_s.at[0], mb_r.at[0], (to, x, y),
            ).start()
            return c

        lax.fori_loop(1, n_dp, send, 0)
        mb[mine] = pmd[mine]

    def make_picks():
        got(mb.at[pl.ds(0, rows - db)], mb_r.at[0])
        k_row = lax.broadcasted_iota(jnp.int32, (LANES, LANES), 0)
        k_col = lax.broadcasted_iota(jnp.int32, (LANES, LANES), 1)
        same = (k_row >> log2(z.tok)) == (k_col >> log2(z.tok))
        count = jnp.where(same, ((k_row & (z.tok - 1)) + 1).astype(F32), 0.0)
        numbers = dot_nn(mb[...], count.astype(BF16)).astype(BF16)
        numbers = dot_nn(mats[1], numbers)
        p_row = lax.broadcasted_iota(jnp.int32, (rows, n_dp * z.tok), 0)
        p_col = lax.broadcasted_iota(jnp.int32, (rows, n_dp * z.tok), 1)
        first = ((p_row & (xb - 1)) >> log2(cap)) * z.tok
        number = (p_col - first + 1).astype(F32)
        for o in range(4):
            found = numbers[:, o * z.tok : o * z.tok + 1]
            pick[o] = onehot(jnp.logical_and(number == found, found > 0.0))

    n_ring = n_z // 2

    def ring_send(b, s):
        block_up = lax.rem(iz + n_z - (s - 1), n_z)
        block_down = lax.rem(iz + (s - 1), n_z)
        some_up, some_down = (0, 4), (0, 4)
        if s == n_ring:
            some_up, some_down = (0, 2), (2, 2)
        a = tb.at[b, pl.ds(*some_up), block_up, ic]
        remote(a, a, bz_s.at[b], bu_r.at[b, s - 1], dev_zup).start()
        a = tb.at[b, pl.ds(*some_down), block_down, ic]
        remote(a, a, bz_s.at[b], bd_r.at[b, s - 1], dev_zdown).start()

    def ring_got(b, s):
        block_up = lax.rem(iz + n_z - s, n_z)
        block_down = lax.rem(iz + s, n_z)
        some_up, some_down = (0, 4), (0, 4)
        if s == n_ring:
            some_up, some_down = (0, 2), (2, 2)
        got(tb.at[b, pl.ds(*some_up), block_up, ic], bu_r.at[b, s - 1])
        got(tb.at[b, pl.ds(*some_down), block_down, ic], bd_r.at[b, s - 1])

    def b_ring(s, b):
        if s == 0:
            got(tb.at[b, pl.ds(0, 3), iz, ic], by_r.at[b])
        else:
            ring_got(b, s)
        if s < n_ring:
            ring_send(b, s + 1)
        else:
            a = tb.at[b, :, :, ic]
            remote(a, a, bs_s.at[b], bs_r.at[b], dev_twin).start()

    def b_select(b):
        got(tb.at[b, :, :, 1 - ic], bs_r.at[b])
        mine = pl.ds(pl.multiple_of(x * xb, 16), xb)

        def one(o, c):
            bsel[b, o] = dot_nn(pick[o], tb[b, o].reshape(n_dp * z.tok, CW)).astype(BF16)
            bx[b, o, mine] = bsel[b, o, mine]

            def send(j, c):
                to = lax.rem(x + j, n_x)
                remote(
                    bsel.at[b, o, pl.ds(pl.multiple_of(to * xb, 16), xb)], bx.at[b, o, mine],
                    bx_s.at[b], bx_r.at[b], (dp, to, y),
                ).start()
                return c

            return lax.fori_loop(1, n_x, send, c)

        lax.fori_loop(0, 4, one, 0)

    def b_place(b):
        got(bx.at[b, :, pl.ds(0, rows - xb)], bx_r.at[b])

        def one(o, c):
            g[z.early + b, o] = dot_nn(mats[0], bx[b, o]).astype(BF16)
            return c

        lax.fori_loop(0, 4, one, 0)

    def b_multiply(b):
        multiply(z.early + b)

    def when_b(t, start, stride, do):
        u = t - start
        on = jnp.logical_and(u >= 0, u < stride * z.late)
        if stride > 1:
            on = jnp.logical_and(on, lax.rem(u + stride * z.late, stride) == 0)
        pl.when(on)(lambda: do(lax.div(u, stride)))

    f0(0, LANES)
    f0(jnp.int32(1), CW)
    spread()
    for q in range(2, min(AHEAD, z.early)):
        f0(jnp.int32(q), CW)
    pt[...] = dot_nt(onehot(t_row == t_col), place_ref[...]).astype(BF16)
    i_row = lax.broadcasted_iota(jnp.int32, (rows, rows), 0)
    i_col = lax.broadcasted_iota(jnp.int32, (rows, rows), 1)

    def reordered(i):
        return (
            ((i & (db - 1)) >> log2(cap)) * xb + (i >> log2(db)) * cap + (i & (cap - 1))
        )

    mats[0] = onehot(i_col == reordered(i_row))
    mats[1] = onehot(i_row == reordered(i_col))


    for i in range(2 + mix):
        wcopy(i).wait()

    t_sel = B_START + B_STEP * n_ring + 1
    t_place = t_sel + B_X
    t_mul = max(t_place + (B_GAP - 1) * (z.late - 1) + 1, mix + LAGS[2] + 2)

    def tick_out(t, c):
        at(t - LAGS[1], f3)
        at(t - LAGS[0], f2)
        at(t, f1)
        pl.when(t + AHEAD < z.early)(functools.partial(f0, t + AHEAD, CW))
        at(t - LAGS[2], f4)
        for s in range(n_ring + 1):
            when_b(t, B_START + B_STEP * s, B_GAP, functools.partial(b_ring, s))
        pl.when(t == B_START)(share_places)
        pl.when(t == t_sel - 1)(make_picks)
        when_b(t, t_sel, B_GAP, b_select)
        when_b(t, t_place, B_GAP, b_place)
        when_b(t, t_mul, 1, b_multiply)
        return c

    lax.fori_loop(0, max(z.early + LAGS[2], t_mul + z.late), tick_out, 0)

    def middle(o):
        back_h = bh[o]
        scaled = gt[o][:, 0:1] * back_h
        gg[o] = (scaled * pu[o]).astype(BF16)
        gu[o] = (scaled * pg[o]).astype(BF16)
        gp[o] = jnp.broadcast_to(
            jnp.sum(hf[o] * back_h, axis=1, keepdims=True), (rows, LANES)
        )

    def partial_rows(o, r, w):
        if w != CW:
            return gp[o]
        part = pl.ds(pl.multiple_of(r * CW, CW), CW)
        return dot_nn(gg[o], wg[:, part]) + dot_nn(gu[o], wu[:, part])

    lo, hi = pl.ds(0, half), pl.ds(half, half)

    def r0(r, w):
        cs = pl.ds(0, w)
        os_[r, :, cs] = partial_rows(far, r, w).astype(BF16)
        remote(os_.at[r, lo, cs], ora.at[r, :, cs], os_s.at[r], ora_r.at[r], dev_down).start()
        remote(os_.at[r, hi, cs], orb.at[r, :, cs], os_s.at[r], orb_r.at[r], dev_up).start()

    def r1(r, w):
        cs = pl.ds(0, w)
        mine = partial_rows(down, r, w)
        got(ora.at[r, :, cs], ora_r.at[r])
        am[r, lo, cs] = (mine[0:half] + ora[r, :, cs].astype(F32)).astype(BF16)
        am[r, hi, cs] = mine[half:].astype(BF16)
        remote(am.at[r, :, cs], arp.at[r, :, cs], a_s.at[r], arp_r.at[r], dev_down).start()
        mine = partial_rows(up, r, w)
        got(orb.at[r, :, cs], orb_r.at[r])
        ap[r, lo, cs] = mine[0:half].astype(BF16)
        ap[r, hi, cs] = (mine[half:] + orb[r, :, cs].astype(F32)).astype(BF16)
        remote(ap.at[r, :, cs], arm.at[r, :, cs], a_s.at[r], arm_r.at[r], dev_up).start()

    def r2(r, w):
        cs = pl.ds(0, w)
        mine = partial_rows(y, r, w)
        got(arp.at[r, :, cs], arp_r.at[r])
        got(arm.at[r, :, cs], arm_r.at[r])
        rd[r, :, cs] = (
            mine + arp[r, :, cs].astype(F32) + arm[r, :, cs].astype(F32)
        ).astype(BF16)
        own = pl.ds(pl.multiple_of(dp * db, 16), db)

        def send(j, c):
            to = lax.rem(dp + j, n_dp)
            remote(
                rd.at[r, pl.ds(pl.multiple_of(to * db, 16), db), cs], rb.at[r, own, cs],
                rd_s.at[r], rb_r.at[r], (to, x, y),
            ).start()
            return c

        lax.fori_loop(1, n_dp, send, 0)
        rb[r, own, cs] = rd[r, own, cs]

    def r3(r, w):
        cs = pl.ds(0, w)
        got(rb.at[r, pl.ds(0, rows - db), cs], rb_r.at[r])
        sx[r, :, cs] = dot_nn(mats[1], rb[r, :, cs]).astype(BF16)
        own = pl.ds(pl.multiple_of(x * xb, 16), xb)

        def send(j, c):
            to = lax.rem(x + j, n_x)
            remote(
                sx.at[r, pl.ds(pl.multiple_of(to * xb, 16), xb), cs], hb.at[r, own, cs],
                sx_s.at[r], hb_r.at[r], (dp, to, y),
            ).start()
            return c

        lax.fori_loop(1, n_x, send, 0)
        hb[r, own, cs] = sx[r, own, cs]

    def r4(r, w):
        got(hb.at[r, pl.ds(0, rows - xb), pl.ds(0, w)], hb_r.at[r])
        if w == CW:
            cols = pl.ds(pl.multiple_of(r * CW, LANES), CW)
            out_tok[:, cols] = dot_nn(pt[...], hb[r]).astype(BF16)
            return
        row = lax.broadcasted_iota(jnp.int32, (rows, LANES), 0)
        lane = lax.broadcasted_iota(jnp.int32, (rows, LANES), 1)
        e = ((row & (xb - 1)) >> log2(cap)) * n_x + (row >> log2(xb))
        vals = jnp.where(e == lane, hb[r, :, 0:LANES].astype(F32), 0.0)
        by_expert = dot_nn(pt[...], vals.astype(BF16))
        e_row = lax.broadcasted_iota(jnp.int32, (LANES, LANES), 0)
        e_col = lax.broadcasted_iota(jnp.int32, (LANES, LANES), 1)
        by_expert = dot_nt(onehot(e_row == e_col), by_expert.astype(BF16))
        e_tok = lax.broadcasted_iota(jnp.int32, (LANES, z.tok), 0)
        out_gate[...] = jnp.concatenate(
            [
                jnp.sum(
                    jnp.where(routes_ref[k : k + 1, :] == e_tok, by_expert, 0.0),
                    axis=0, keepdims=True,
                )
                for k in range(z.top)
            ],
            axis=0,
        ).astype(BF16)

    def back(t, do):
        pl.when(jnp.logical_and(t >= 0, t < mix))(functools.partial(do, t, CW))
        pl.when(t == mix)(functools.partial(do, t, LANES))

    def drain_out(q, w):
        cs = pl.ds(0, w)
        left(sel.at[q, pl.ds(0, rows - xb), cs], xs.at[q])
        left(sd.at[q, pl.ds(0, rows - db), cs], ds_.at[q])
        left(g.at[q, pl.ds(0, 3), :, cs], ys.at[q])

    def drain_all_out():
        drain_out(0, LANES)
        for q in range(1, z.early):
            drain_out(q, CW)
        for b in range(z.late):
            left(tb.at[b, pl.ds(0, 3), 0, 0], by_s.at[b])
            left(tb.at[b, :, pl.ds(0, n_z - 1), 0], bz_s.at[b])
            left(tb.at[b, :, :, 0], bs_s.at[b])
            left(bx.at[b, :, pl.ds(0, rows - xb)], bx_s.at[b])
        left(pmy.at[pl.ds(0, 3)], pm_s.at[0])
        left(mb.at[pl.ds(0, rows - db)], mb_s.at[0])

    def rest():
        middle(y)
        grad_down(z.early - 1)

    def tick_back(t, c):
        back(t - 2, r1)
        back(t, r0)
        pl.when(t == 3)(rest)
        back(t - 4, r2)
        back(t - 6, r3)
        back(t - 8, r4)
        pl.when(t == 5)(drain_all_out)
        return c

    middle(far)
    r0(0, CW)
    r0(1, CW)
    middle(down)
    middle(up)
    lax.fori_loop(2, z.ret + 8, tick_back, 0)

    def drain_back(r, w):
        cs = pl.ds(0, w)
        left(os_.at[r, :, cs], os_s.at[r])
        left(g.at[r, pl.ds(0, 2), :, cs], a_s.at[r])
        left(rd.at[r, pl.ds(0, rows - db), cs], rd_s.at[r])
        left(sx.at[r, pl.ds(0, rows - xb), cs], sx_s.at[r])

    for j in range(mix):
        down_copy(j).wait()
    for r in range(mix):
        drain_back(r, CW)
    drain_back(mix, LANES)


def hand_over(tok_in, gate_in, down_in, tok_out, gate_out, down_out, tok, down, sem):
    parts = [(tok_in, tok, tok_out)]
    step = down.shape[0] // 4
    for i in range(4):
        part = pl.ds(i * step, step)
        parts.append((down_in.at[part], down.at[part], down_out.at[part]))
    reads = [
        pltpu.make_async_copy(a, b, sem.at[0, i]) for i, (a, b, _) in enumerate(parts)
    ]
    writes = [
        pltpu.make_async_copy(b, c, sem.at[1, i]) for i, (_, b, c) in enumerate(parts)
    ]
    for read in reads:
        read.start()
    gate_out[...] = gate_in[...]
    for read, write in zip(reads, writes):
        read.wait()
        write.start()
    for write in writes:
        write.wait()


def body(cap, tokens, out_grad, routes, gates, w_gate, w_up, w_down):
    z = Sizes(
        late=min(LATE, tokens.shape[1] // CW - 1),
        n_dp=lax.axis_size("dp"), n_x=lax.axis_size("expert"), tok=tokens.shape[0],
        top=routes.shape[1], cap=cap, width=tokens.shape[1], ff=w_gate.shape[2],
    )
    assert lax.axis_size("tensor") == 4 and z.width % CW == 0
    rows, half, fwd, ret, mix = z.rows, z.rows // 2, z.fwd, z.ret, z.mix
    vm = pltpu.VMEM
    sem = pltpu.SemaphoreType.DMA
    scratch = [
        vm(routes.T.shape, routes.dtype),
        vm(tokens.shape, tokens.dtype),
        vm(out_grad.shape, out_grad.dtype),
        sem((3,)),
        vm((z.ff, z.width), F32),
        vm((rows, z.tok), BF16),
        vm((fwd, z.tok, CW), BF16),
        vm((fwd, rows, CW), BF16),
        vm((fwd, rows, CW), BF16),
        vm((fwd, rows, CW), BF16),
        vm((fwd, 4, rows, CW), BF16),
        vm((z.ff, z.width), BF16),
        vm((z.ff, z.width), BF16),
        vm((mix, z.ff, CW), BF16),
        vm((4, rows, z.ff), F32),
        vm((4, rows, z.ff), F32),
        vm((4, rows, z.ff), F32),
        vm((4, z.ff, rows), BF16),
        vm((4, rows, z.ff), F32),
        vm((4, rows, LANES), F32),
        vm((4, rows, z.ff), BF16),
        vm((4, rows, z.ff), BF16),
        vm((4, rows, LANES), F32),
        vm((2, rows, rows), BF16),
        vm((z.tok, rows), BF16),
        vm((ret, rows, CW), BF16),
        vm((ret, half, CW), BF16),
        vm((ret, half, CW), BF16),
        vm((ret, rows, CW), BF16),
        vm((ret, rows, CW), BF16),
        vm((ret, rows, CW), BF16),
        vm((ret, rows, CW), BF16),
        vm((ret, rows, CW), BF16),
        vm((ret, rows, CW), BF16),
        vm((ret, rows, CW), BF16),
        vm((ret, rows, CW), BF16),
        vm((z.late, 4, z.n_z, 2, z.tok, CW), BF16),
        vm((4, rows, LANES), BF16),
        vm((rows, LANES), BF16),
        vm((rows, LANES), BF16),
        vm((4, rows, z.n_dp * z.tok), BF16),
        vm((z.late, 4, rows, CW), BF16),
        vm((z.late, 4, rows, CW), BF16),
        sem((z.late,)), sem((z.late,)),
        sem((z.late, z.n_z // 2)), sem((z.late, z.n_z // 2)), sem((z.late,)),
        sem((z.late,)), sem((z.late,)), sem((z.late,)), sem((z.late,)),
        sem((1,)), sem((1,)), sem((1,)), sem((1,)),
        sem((2 + mix,)),
        sem((mix,)),
    ] + [sem((fwd,))] * 9 + [sem((ret,))] * 10
    vmem = pl.BlockSpec(memory_space=pltpu.VMEM)
    hbm = pl.BlockSpec(memory_space=pl.ANY)
    grad_tokens, grad_gate, grad_down = pl.pallas_call(
        functools.partial(kernel, z),
        out_shape=(
            jax.ShapeDtypeStruct((z.tok, z.width), BF16),
            jax.ShapeDtypeStruct((z.top, z.tok), BF16),
            jax.ShapeDtypeStruct((z.ff, z.width), F32),
        ),
        in_specs=[hbm, vmem] + [hbm] * 5,
        out_specs=(vmem, vmem, hbm),
        scratch_shapes=scratch,
        compiler_params=pltpu.CompilerParams(
            collective_id=0, has_side_effects=True, vmem_limit_bytes=60 * 1024 * 1024
        ),
    )(routes.T, gates.T, tokens, out_grad, w_gate[0].T, w_up[0].T, w_down[0])
    results = (grad_tokens, grad_gate, grad_down)
    grad_tokens, grad_gate, grad_down = pl.pallas_call(
        hand_over,
        out_shape=tuple(jax.ShapeDtypeStruct(r.shape, r.dtype) for r in results),
        in_specs=[hbm, vmem, hbm],
        out_specs=(hbm, vmem, hbm),
        scratch_shapes=[
            vm(grad_tokens.shape, BF16), vm(grad_down.shape, F32), sem((2, 5)),
        ],
    )(*results)
    return grad_tokens, grad_gate.T, grad_down[None]


def solution(mesh, cap=4):
    tokens = P(("dp", "expert", "tensor"), None)
    return jax.shard_map(
        functools.partial(body, cap),
        mesh=mesh,
        in_specs=(
            tokens, tokens, tokens, tokens,
            P(("dp", "expert"), None, "tensor"),
            P(("dp", "expert"), None, "tensor"),
            P(("dp", "expert"), "tensor", None),
        ),
        out_specs=(tokens, tokens, P(("dp", "expert"), "tensor", None)),
        check_vma=False,
    )
```
